32 devices in a mesh: groups: 2 (over x), wide: 16 (over z, y, core).
Axes of the slice: x: 2, y: 2, z: 4, core: 2. Of those that a mesh axis runs over, the one named last changes fastest.
Arguments:
- gamma: bfloat16 [4, 11008, 512], P('groups', 'wide'), parts along dimension 0, may hold values from -6 to 6
- coefficients: bfloat16 [6144, 11008], P('wide'), may hold values from -0.0546875 to 0.0546875
- owners: int32 [2048, 1], P('wide'), may hold values from 0 to 15; in each aligned block of 128 rows (0 to 127, 128 to 255, ...) at most 16 rows name the same one
Outputs:
- owned_blocks: bfloat16 [16, 16, 32, 6, 512], P('wide', None, 'groups'), parts along dimension 2
- owned_ids: int32 [16, 32, 16], P('wide', 'groups'), parts along dimension 1
The draws below stay inside these ranges and needn't reach their ends.
There are 2 independent parts, one for each index of `groups`. The reference program is written for one: setup_inputs(seed, part) draws one part's arguments, and reference() takes and returns one part's arrays. A program takes and returns all parts, laid end to end along the dimension named above; an argument that names none is the same for every part. Nothing has to cross between parts.
Inputs may be any that keep to these rules, and one draw needn't show every extreme that they name: `owners`: among the 128 blocks of one source device (aligned blocks of rows), no owner is named more than 16 times, a bound that some block reaches; every owner owns some block.
All inputs are finite; a program needn't handle non-finite values.
Results may differ from the reference program's by a relative error of at most 0.001.
Values may be sent and summed in bfloat16 or wider, within the bound.
No kernel may reach another device: no remote copies, remote signals or barrier semaphores. Data moves between devices by JAX's collectives and lax.ppermute only.
A program may use at most 128 MiB of HBM per device.

```python
import math
import jax
import jax.numpy as jnp
import numpy as np
from jax import lax

NOCC = 2
NV = 11008
BS = 3
BLK_DEV = 128
NAUX = 512
NBLK = 2048
NAO = 6144
SLOTS = 16
N_WIDE = 16


def level_of(key, extent, pieces, smallest, high):
    level = 1.0
    for axis_at, shards_of in pieces:
        draws = jax.random.uniform(jax.random.fold_in(jax.random.fold_in(key, 6), axis_at), (shards_of,), jnp.float32, smallest / len(pieces), high / len(pieces))
        level = level * jnp.repeat(jnp.exp(draws), extent[axis_at] // shards_of).reshape((-1,) + (1,) * (len(extent) - 1 - axis_at))
    return level


def routed_block(own_key, own, number, rows, number_of, top, most, skew):
    sequence = jax.random.permutation(own_key, number_of)
    crowded, common = load_shares(number_of, rows * top, most, skew, True), load_shares(number_of, rows * top, most, skew, False)
    places = jnp.arange(number_of)

    def named(tallies, rotation):
        used = int((tallies > 0).sum())
        fixed = max(1, used // 4)
        moved = fixed + (places - fixed + rotation * (used - fixed)) % max(1, number_of - fixed)
        return jnp.zeros((number_of,), jnp.int32).at[sequence[jnp.where(places < fixed, places, moved)]].set(jnp.asarray(tallies, jnp.int32))

    tallies = jnp.where(number % 4 == 0, named(crowded, number // 4), named(common, number - number // 4 - 1))
    mixed = jax.random.permutation(jax.random.fold_in(own, 3), number_of)
    source_of, sink = mixed[0:number_of // 2 * 2:2], mixed[1:number_of // 2 * 2:2]
    slack = jnp.minimum(tallies[source_of] - 1, most - tallies[sink]) // 2
    slack = jnp.where((source_of == sequence[0]) | (sink == sequence[0]) | (tallies[sink] == 0), 0, jnp.maximum(slack, 0))
    moved = jax.random.randint(jax.random.fold_in(own, 4), (number_of // 2,), 0, 1 << 20) % (slack + 1)
    tallies = tallies.at[source_of].add(-moved).at[sink].add(moved)
    items = jnp.searchsorted(jnp.cumsum(tallies), jnp.arange(rows * top), side="right").astype(jnp.int32)
    listing = items.reshape(top, rows).T
    listing = listing[jax.random.permutation(jax.random.fold_in(own, 1), rows)]
    rotation = jax.random.randint(jax.random.fold_in(own, 2), (rows, 1), 0, top)
    return jnp.take_along_axis(listing, (jnp.arange(top)[None, :] + rotation) % top, axis=1)


def load_shares(number_of, total, most, lean, full):
    portions = [(1 << 20) // math.isqrt(standing ** lean) + 1 for standing in range(1, number_of + 1)]
    largest = most if full else min(most, max(-(-total // number_of), total * portions[0] // sum(portions)))
    least = 1 if total - largest >= number_of - 1 else 0
    given, rest = [largest] + [least] * (number_of - 1), total - largest - least * (number_of - 1)
    while rest > 0:
        free = [i for i in range(1, number_of) if given[i] < largest] or [i for i in range(1, number_of) if given[i] < most]
        mass, budget = sum([portions[i] for i in free]), rest
        for i in free:
            extra = min(most - given[i], max(1, budget * portions[i] // mass), rest)
            given[i] = given[i] + extra
            rest = rest - extra
    return np.array(given)


def scatter_about(stream_key, dims, deviation, limit, pieces=(), kind=jnp.bfloat16):
    loudness = level_of(stream_key, dims, pieces, -0.22, 0.18) if pieces else 1.0
    result = jax.random.normal(stream_key, dims, jnp.float32) * deviation * loudness
    return jnp.minimum(jnp.maximum(result, -limit), limit).astype(kind)


def setup_inputs(seed: int = 0, part: int = 0) -> dict:
    keys = jax.random.split(jax.random.key(seed), 4)
    part_keys = jax.random.split(jax.random.fold_in(keys[3], part), 4)
    gamma = scatter_about(part_keys[0], (NOCC, NV, NAUX), 1.0, 6.0, ((1, 16),))
    coefficients = scatter_about(keys[1], (NAO, NV), NV ** -0.5, 0.0546875, ((0, 16),))
    owners_keys = jax.random.split(jax.random.fold_in(keys[2], 1), NBLK // BLK_DEV)
    owners_turns = jax.random.permutation(jax.random.fold_in(keys[2], 3), NBLK // BLK_DEV)
    owners = jax.vmap(lambda own, number: routed_block(jax.random.fold_in(keys[2], 2), own, number, BLK_DEV, N_WIDE, 1, SLOTS, 2))(owners_keys, owners_turns).reshape((NBLK, 1))
    return {"gamma": gamma, "coefficients": coefficients, "owners": owners}


def reference(gamma, coefficients, owners):
    def one_orbital(slab):
        return jnp.dot(coefficients, slab, preferred_element_type=jnp.float32).astype(jnp.bfloat16)

    back = lax.map(one_orbital, gamma)
    blocks = back.reshape(NOCC, NBLK, BS, NAUX).transpose(1, 0, 2, 3).reshape(NBLK, NOCC * BS, NAUX)
    owner_grid = owners[:, 0].reshape(N_WIDE, BLK_DEV).astype(jnp.int32)
    same = owner_grid[:, :, None] == owner_grid[:, None, :]
    lower = jnp.arange(BLK_DEV)[:, None] > jnp.arange(BLK_DEV)[None, :]
    rank = jnp.sum((same & lower[None, :, :]).astype(jnp.int32), axis=2)
    source = jnp.arange(N_WIDE, dtype=jnp.int32)[:, None]
    target = (owner_grid * (N_WIDE * SLOTS) + source * SLOTS + rank).reshape(-1).astype(jnp.int32)
    filled = jnp.zeros((N_WIDE * N_WIDE * SLOTS, NOCC * BS, NAUX), jnp.bfloat16).at[target].set(blocks)
    labels = jnp.full((N_WIDE * N_WIDE * SLOTS,), -1, jnp.int32).at[target].set(jnp.arange(NBLK, dtype=jnp.int32))
    return filled.reshape(N_WIDE, N_WIDE, SLOTS, NOCC * BS, NAUX), labels.reshape(N_WIDE, N_WIDE, SLOTS)
```

```python
import jax
import jax.numpy as jnp
from jax import lax
from jax.sharding import PartitionSpec as P


def local(gamma, coefficients, owners):
    count = lax.axis_size("wide")
    blocks_here = owners.shape[0]
    slots = max(2, 2 * blocks_here // count)
    rows = coefficients.shape[0]
    block_rows = rows // blocks_here
    norb, _, naux = gamma.shape
    parts = 2
    width = naux // parts

    gathered = [
        [
            lax.all_gather(
                gamma[i, :, j * width : (j + 1) * width], "wide", axis=0, tiled=True
            )
            for j in range(parts)
        ]
        for i in range(norb)
    ]

    owner_col = owners[:, 0]
    same = owner_col[:, None] == owner_col[None, :]
    lower = jnp.arange(blocks_here)[:, None] > jnp.arange(blocks_here)[None, :]
    rank = jnp.sum((same & lower).astype(jnp.int32), axis=1)
    target = owner_col * slots + rank
    select = jnp.arange(count * slots, dtype=jnp.int32)[:, None] == target[None, :]
    global_ids = lax.axis_index("wide") * blocks_here + jnp.arange(blocks_here, dtype=jnp.int32)
    labels = jnp.sum(jnp.where(select, global_ids[None, :] + 1, 0), axis=1) - 1
    labels = labels.reshape(count, slots)
    ids = lax.all_to_all(labels, "wide", split_axis=0, concat_axis=0, tiled=True)

    row_at = jnp.arange(rows, dtype=jnp.int32)
    out_at = jnp.arange(count * block_rows * slots, dtype=jnp.int32)
    row_key = jnp.repeat(target, block_rows) * block_rows + row_at % block_rows
    out_key = (
        out_at // (block_rows * slots) * slots + out_at % slots
    ) * block_rows + out_at // slots % block_rows
    place = (out_key[:, None] == row_key[None, :]).astype(jnp.bfloat16)

    arrived = []
    for i in range(norb):
        row = []
        for j in range(parts):
            back = jnp.dot(
                coefficients, gathered[i][j], preferred_element_type=jnp.float32
            ).astype(jnp.bfloat16)
            out = jnp.dot(place, back, preferred_element_type=jnp.float32)
            out = out.astype(jnp.bfloat16).reshape(count, block_rows, slots, width)
            row.append(
                lax.all_to_all(out, "wide", split_axis=0, concat_axis=0, tiled=True)
            )
        arrived.append(jnp.concatenate(row, axis=3))
    placed = jnp.stack(arrived, axis=1)
    placed = placed.reshape(count, norb * block_rows, slots, naux).transpose(0, 2, 1, 3)
    return placed[None], ids[None]


def solution(mesh):
    placed = (P("groups", "wide", None), P("wide", None), P("wide", None))
    return jax.shard_map(
        local,
        mesh=mesh,
        in_specs=placed,
        out_specs=(P("wide", None, "groups", None, None), P("wide", "groups", None)),
        check_vma=False,
    )
```

```python
import jax
import jax.numpy as jnp
from jax import lax
from jax.sharding import PartitionSpec as P

GRID_RING = [0, 1, 3, 5, 7, 6, 4, 2]
LAG = 3


def routing(owners, count, slots, block_rows):
    blocks_here = owners.shape[0]
    rows = blocks_here * block_rows
    owner_col = owners[:, 0]
    same = owner_col[:, None] == owner_col[None, :]
    lower = jnp.arange(blocks_here)[:, None] > jnp.arange(blocks_here)[None, :]
    rank = jnp.sum((same & lower).astype(jnp.int32), axis=1)
    target = owner_col * slots + rank
    select = jnp.arange(count * slots, dtype=jnp.int32)[:, None] == target[None, :]
    global_ids = lax.axis_index("wide") * blocks_here + jnp.arange(blocks_here, dtype=jnp.int32)
    labels = jnp.sum(jnp.where(select, global_ids[None, :] + 1, 0), axis=1) - 1
    row_at = jnp.arange(rows, dtype=jnp.int32)
    out_at = jnp.arange(count * block_rows * slots, dtype=jnp.int32)
    row_key = jnp.repeat(target, block_rows) * block_rows + row_at % block_rows
    out_key = (
        out_at // (block_rows * slots) * slots + out_at % slots
    ) * block_rows + out_at // slots % block_rows
    place = (out_key[:, None] == row_key[None, :]).astype(jnp.bfloat16)
    return labels.reshape(count, slots), place


def local(gamma, coefficients, owners):
    count = lax.axis_size("wide")
    blocks_here = owners.shape[0]
    slots = max(2, 2 * blocks_here // count)
    rows, nvirt = coefficients.shape
    block_rows = rows // blocks_here
    norb, depth, naux = gamma.shape
    chips = count // 2
    half = naux // 2

    labels, place = routing(owners, count, slots, block_rows)

    def send(i_back):
        out = jnp.dot(place, i_back, preferred_element_type=jnp.float32)
        out = out.astype(jnp.bfloat16).reshape(count, block_rows, slots, naux)
        return lax.all_to_all(out, "wide", split_axis=0, concat_axis=0, tiled=True)

    ids = lax.all_to_all(labels, "wide", split_axis=0, concat_axis=0, tiled=True)

    if chips != len(GRID_RING):
        gathered = lax.all_gather(gamma, "wide", axis=1, tiled=True)
        arrived = [
            send(
                jnp.dot(
                    coefficients, gathered[i], preferred_element_type=jnp.float32
                ).astype(jnp.bfloat16)
            )
            for i in range(norb)
        ]
        placed = jnp.concatenate(arrived, axis=1).transpose(0, 2, 1, 3)
        return placed[None], ids[None]

    ring = GRID_RING
    me = lax.axis_index("wide")
    core = me % 2
    ring_at = jnp.asarray(ring, jnp.int32)
    place_of = jnp.asarray([ring.index(c) for c in range(chips)], jnp.int32)
    here = place_of[me // 2]
    swap = [(d, d ^ 1) for d in range(count)]
    by_source = coefficients.reshape(rows, count, depth).transpose(1, 0, 2)

    def shift(step):
        return [
            (2 * ring[p] + k, 2 * ring[(p + step) % chips] + k)
            for p in range(chips)
            for k in range(2)
        ]

    pieces = {}
    total = {}
    for i in range(norb):
        for d in range(2):
            pieces[i, d] = [gamma[i, :, d * half : (d + 1) * half]]
            total[i, d] = jnp.zeros((rows, half), jnp.float32)
    for tick in range(chips - 1 + LAG * (norb - 1)):
        for i in range(norb):
            t = tick - LAG * i
            if not 0 <= t < chips - 1:
                continue
            for d in range(2):
                block = pieces[i, d][t]
                if i:
                    ahead = min(chips - 1, t + LAG)
                    block, pieces[i - 1, d][ahead] = lax.optimization_barrier(
                        (block, pieces[i - 1, d][ahead])
                    )
                pieces[i, d].append(lax.ppermute(block, "wide", shift(1 - 2 * d)))

    arrived = []
    for i in range(norb):
        outs = []
        for d in range(2):
            acc = None
            for t in range(chips):
                own = pieces[i, d][t]
                other = lax.ppermute(own, "wide", swap)
                chip = ring_at[(here - t * (1 - 2 * d)) % chips]
                for block, which in ((own, core), (other, 1 - core)):
                    left = lax.dynamic_index_in_dim(by_source, 2 * chip + which, 0, False)
                    term = jnp.dot(left, block, preferred_element_type=jnp.float32)
                    acc = term if acc is None else acc + term
            outs.append(acc.astype(jnp.bfloat16))
        arrived.append(send(jnp.concatenate(outs, axis=1)))
    placed = jnp.concatenate(arrived, axis=1).transpose(0, 2, 1, 3)
    return placed[None], ids[None]


def solution(mesh):
    placed = (P("groups", "wide", None), P("wide", None), P("wide", None))
    return jax.shard_map(
        local,
        mesh=mesh,
        in_specs=placed,
        out_specs=(P("wide", None, "groups", None, None), P("wide", "groups", None)),
        check_vma=False,
    )
```

```python
import jax
import jax.numpy as jnp
from jax import lax
from jax.experimental import pallas as pl
from jax.experimental.pallas import tpu as pltpu
from jax.sharding import PartitionSpec as P

GRID_CHIPS = 8
CHUNK = 1536


def ring_chip(at):
    at = at % GRID_CHIPS
    back = 2 * ((GRID_CHIPS - at) % GRID_CHIPS)
    up = 2 * at - 1
    if isinstance(at, int):
        return up if 1 <= at <= GRID_CHIPS // 2 else back
    return jnp.where((at >= 1) & (at <= GRID_CHIPS // 2), up, back)


def ring_place(chip):
    z, y = chip // 2, chip % 2
    return jnp.where(y == 1, 1 + z, (GRID_CHIPS - z) % GRID_CHIPS)


def routing(owners, count, slots, block_rows):
    blocks_here = owners.shape[0]
    rows = blocks_here * block_rows
    owner_col = owners[:, 0]
    same = owner_col[:, None] == owner_col[None, :]
    lower = jnp.arange(blocks_here)[:, None] > jnp.arange(blocks_here)[None, :]
    rank = jnp.sum((same & lower).astype(jnp.int32), axis=1)
    target = owner_col * slots + rank
    select = jnp.arange(count * slots, dtype=jnp.int32)[:, None] == target[None, :]
    global_ids = lax.axis_index("wide") * blocks_here + jnp.arange(blocks_here, dtype=jnp.int32)
    labels = jnp.sum(jnp.where(select, global_ids[None, :] + 1, 0), axis=1) - 1
    row_at = jnp.arange(rows, dtype=jnp.int32)
    out_at = jnp.arange(count * block_rows * slots, dtype=jnp.int32)
    row_key = jnp.repeat(target, block_rows) * block_rows + row_at % block_rows
    out_key = (
        out_at // (block_rows * slots) * slots + out_at % slots
    ) * block_rows + out_at // slots % block_rows
    place = (out_key[:, None] == row_key[None, :]).astype(jnp.bfloat16)
    return labels.reshape(count, slots), place


def product_kernel(c_hbm, g_hbm, place_ref, out_ref, c_buf, g_buf, total, c_sem, g_sem):
    depth = c_hbm.shape[1]
    starts = list(range(0, depth, CHUNK))

    def c_copy(k, size):
        at = pl.ds(k * CHUNK, size)
        return pltpu.make_async_copy(c_hbm.at[:, at], c_buf.at[:, at], c_sem.at[k])

    def g_copy(k, size):
        at = pl.ds(k * CHUNK, size)
        return pltpu.make_async_copy(g_hbm.at[at, :], g_buf.at[at, :], g_sem.at[k])

    for k, start in enumerate(starts):
        size = min(CHUNK, depth - start)
        c_copy(k, size).start()
        g_copy(k, size).start()

    total[...] = jnp.zeros_like(total)

    def step(k, size):
        c_copy(k, size).wait()
        g_copy(k, size).wait()
        at = pl.ds(pl.multiple_of(k * CHUNK, CHUNK), size)
        total[...] += jnp.dot(
            c_buf[:, at], g_buf[at, :], preferred_element_type=jnp.float32
        )

    whole = depth // CHUNK
    pl.loop(0, whole)(lambda k: step(k, CHUNK))
    if depth % CHUNK:
        step(whole, depth % CHUNK)
    back = total[...].astype(jnp.bfloat16)
    out_ref[...] = jnp.dot(
        place_ref[...], back, preferred_element_type=jnp.float32
    ).astype(jnp.bfloat16)


def product(coefficients, gathered, place):
    rows, depth = coefficients.shape
    width = gathered.shape[1]
    chunks = -(-depth // CHUNK)
    return pl.pallas_call(
        product_kernel,
        out_shape=jax.ShapeDtypeStruct((place.shape[0], width), jnp.bfloat16),
        in_specs=[
            pl.BlockSpec(memory_space=pl.ANY),
            pl.BlockSpec(memory_space=pl.ANY),
            pl.BlockSpec(memory_space=pltpu.VMEM),
        ],
        out_specs=pl.BlockSpec(memory_space=pltpu.VMEM),
        scratch_shapes=[
            pltpu.VMEM((rows, depth), jnp.bfloat16),
            pltpu.VMEM((depth, width), jnp.bfloat16),
            pltpu.VMEM((rows, width), jnp.float32),
            pltpu.SemaphoreType.DMA((chunks,)),
            pltpu.SemaphoreType.DMA((chunks,)),
        ],
        compiler_params=pltpu.CompilerParams(vmem_limit_bytes=40 << 20),
        cost_estimate=pl.CostEstimate(
            flops=2 * rows * depth * width,
            bytes_accessed=2 * depth * (rows + width),
            transcendentals=0,
        ),
    )(coefficients, gathered, place)


def local(gamma, coefficients, owners):
    count = lax.axis_size("wide")
    blocks_here = owners.shape[0]
    slots = max(2, 2 * blocks_here // count)
    rows, nvirt = coefficients.shape
    block_rows = rows // blocks_here
    norb, depth, naux = gamma.shape
    chips = count // 2
    width = norb * naux

    labels, place = routing(owners, count, slots, block_rows)
    ids = lax.all_to_all(labels, "wide", split_axis=0, concat_axis=0, tiled=True)

    def send(out):
        out = out.reshape(count, block_rows, slots, out.shape[1])
        return lax.all_to_all(out, "wide", split_axis=0, concat_axis=0, tiled=True)

    def select(back):
        out = jnp.dot(place, back, preferred_element_type=jnp.float32)
        return out.astype(jnp.bfloat16)

    flat = jnp.concatenate([gamma[i] for i in range(norb)], axis=1)
    if chips != GRID_CHIPS:
        gathered = lax.all_gather(flat, "wide", axis=0, tiled=True)
        back = jnp.dot(coefficients, gathered, preferred_element_type=jnp.float32)
        arrived = send(select(back.astype(jnp.bfloat16)))
    else:
        rest = 128
        main = width - 2 * rest
        gathered = lax.all_gather(flat[:, :main], "wide", axis=0, tiled=True)

        me = lax.axis_index("wide")
        core = me % 2
        here = ring_place(me // 2)
        swap = [(d, d ^ 1) for d in range(count)]
        by_source = coefficients.reshape(rows, count, depth).transpose(1, 0, 2)
        outs = []
        for d, way in enumerate((1, -1)):
            shift = [
                (2 * ring_chip(p) + k, 2 * ring_chip(p + way) + k)
                for p in range(chips)
                for k in range(2)
            ]
            own = flat[:, main + d * rest : main + (d + 1) * rest]
            acc = jnp.zeros((rows, rest), jnp.float32)
            for t in range(chips):
                if t:
                    own = lax.ppermute(own, "wide", shift)
                other = lax.ppermute(own, "wide", swap)
                chip = ring_chip(here - t * way + chips)
                for block, which in ((own, core), (other, 1 - core)):
                    left = lax.dynamic_index_in_dim(by_source, 2 * chip + which, 0, False)
                    acc += jnp.dot(left, block, preferred_element_type=jnp.float32)
            outs.append(acc.astype(jnp.bfloat16))
        small = send(select(jnp.concatenate(outs, axis=1)))
        arrived = jnp.concatenate(
            [send(product(coefficients, gathered, place)), small], axis=3
        )
    placed = jnp.concatenate(
        [arrived[..., i * naux : (i + 1) * naux] for i in range(norb)], axis=1
    )
    return placed.transpose(0, 2, 1, 3)[None], ids[None]


def solution(mesh):
    placed = (P("groups", "wide", None), P("wide", None), P("wide", None))
    return jax.shard_map(
        local,
        mesh=mesh,
        in_specs=placed,
        out_specs=(P("wide", None, "groups", None, None), P("wide", "groups", None)),
        check_vma=False,
    )
```

```python
import jax
import jax.numpy as jnp
from jax import lax
from jax.experimental import pallas as pl
from jax.experimental.pallas import tpu as pltpu
from jax.sharding import PartitionSpec as P

CHUNK = 1536


def routing(owners, count, slots, block_rows):
    blocks_here = owners.shape[0]
    rows = blocks_here * block_rows
    owner_col = owners[:, 0]
    same = owner_col[:, None] == owner_col[None, :]
    lower = jnp.arange(blocks_here)[:, None] > jnp.arange(blocks_here)[None, :]
    rank = jnp.sum((same & lower).astype(jnp.int32), axis=1)
    target = owner_col * slots + rank
    select = jnp.arange(count * slots, dtype=jnp.int32)[:, None] == target[None, :]
    global_ids = lax.axis_index("wide") * blocks_here + jnp.arange(blocks_here, dtype=jnp.int32)
    labels = jnp.sum(jnp.where(select, global_ids[None, :] + 1, 0), axis=1) - 1
    row_at = jnp.arange(rows, dtype=jnp.int32)
    out_at = jnp.arange(count * block_rows * slots, dtype=jnp.int32)
    row_key = jnp.repeat(target, block_rows) * block_rows + row_at % block_rows
    out_key = (
        out_at // (block_rows * slots) * slots + out_at % slots
    ) * block_rows + out_at // slots % block_rows
    place = (out_key[:, None] == row_key[None, :]).astype(jnp.bfloat16)
    return labels.reshape(count, slots), place


def product_kernel(c_hbm, g_hbm, place_ref, out_ref, c_buf, g_buf, total, c_sem, g_sem):
    depth = c_hbm.shape[1]
    norb = g_hbm.shape[0]
    count, planes, slots, naux = out_ref.shape
    starts = list(range(0, depth, CHUNK))

    def c_copy(k, size):
        at = pl.ds(k * CHUNK, size)
        return pltpu.make_async_copy(c_hbm.at[:, at], c_buf.at[:, at], c_sem.at[k])

    def g_copy(k, size):
        at = pl.ds(k * CHUNK, size)
        return pltpu.make_async_copy(g_hbm.at[:, at, :], g_buf.at[:, at, :], g_sem.at[k])

    for k, start in enumerate(starts):
        size = min(CHUNK, depth - start)
        c_copy(k, size).start()
        g_copy(k, size).start()

    total[...] = jnp.zeros_like(total)

    def step(k, size):
        c_copy(k, size).wait()
        g_copy(k, size).wait()
        at = pl.ds(pl.multiple_of(k * CHUNK, CHUNK), size)
        for i in range(norb):
            total[i] += jnp.dot(
                c_buf[:, at], g_buf[i, at, :], preferred_element_type=jnp.float32
            )

    whole = depth // CHUNK
    pl.loop(0, whole)(lambda k: step(k, CHUNK))
    if depth % CHUNK:
        step(whole, depth % CHUNK)
    for i in range(norb):
        out = jnp.dot(
            place_ref[...], total[i].astype(jnp.bfloat16), preferred_element_type=jnp.float32
        ).astype(jnp.bfloat16)
        plane = pl.ds(i * (planes // norb), planes // norb)
        out_ref[:, plane] = out.reshape(count, planes // norb, slots, naux)


def product(coefficients, gathered, place, slots):
    rows, depth = coefficients.shape
    norb, _, naux = gathered.shape
    chunks = -(-depth // CHUNK)
    out_rows = place.shape[0] * norb
    count = lax.axis_size("wide")
    planes = out_rows // (count * slots)
    return pl.pallas_call(
        product_kernel,
        out_shape=jax.ShapeDtypeStruct((count, planes, slots, naux), jnp.bfloat16),
        in_specs=[
            pl.BlockSpec(memory_space=pltpu.HBM),
            pl.BlockSpec(memory_space=pltpu.HBM),
            pl.BlockSpec(memory_space=pltpu.VMEM),
        ],
        out_specs=pl.BlockSpec(memory_space=pltpu.VMEM),
        scratch_shapes=[
            pltpu.VMEM((rows, depth), jnp.bfloat16),
            pltpu.VMEM((norb, depth, naux), jnp.bfloat16),
            pltpu.VMEM((norb, rows, naux), jnp.float32),
            pltpu.SemaphoreType.DMA((chunks,)),
            pltpu.SemaphoreType.DMA((chunks,)),
        ],
        compiler_params=pltpu.CompilerParams(vmem_limit_bytes=48 << 20),
        cost_estimate=pl.CostEstimate(
            flops=2 * rows * depth * norb * naux,
            bytes_accessed=2 * depth * (rows + norb * naux),
            transcendentals=0,
        ),
    )(coefficients, gathered, place)


def local(gamma, coefficients, owners):
    count = lax.axis_size("wide")
    blocks_here = owners.shape[0]
    slots = max(2, 2 * blocks_here // count)
    block_rows = coefficients.shape[0] // blocks_here
    norb, depth, naux = gamma.shape

    gathered = lax.all_gather(gamma, "wide", axis=1, tiled=True)
    labels, place = routing(owners, count, slots, block_rows)
    ids = lax.all_to_all(labels, "wide", split_axis=0, concat_axis=0, tiled=True)
    if slots % 16 == 0:
        out = product(coefficients, gathered, place, slots)
    else:
        back = jnp.einsum(
            "ra,ian->irn", coefficients, gathered, preferred_element_type=jnp.float32
        ).astype(jnp.bfloat16)
        out = jnp.einsum("tr,irn->itn", place, back, preferred_element_type=jnp.float32)
        out = out.astype(jnp.bfloat16).reshape(norb, count, block_rows, slots, naux)
        out = out.transpose(1, 0, 2, 3, 4).reshape(count, norb * block_rows, slots, naux)
    placed = lax.all_to_all(out, "wide", split_axis=0, concat_axis=0, tiled=True)
    return placed.transpose(0, 2, 1, 3)[None], ids[None]


def solution(mesh):
    placed = (P("groups", "wide", None), P("wide", None), P("wide", None))
    return jax.shard_map(
        local,
        mesh=mesh,
        in_specs=placed,
        out_specs=(P("wide", None, "groups", None, None), P("wide", "groups", None)),
        check_vma=False,
    )
```

```python
import math

import jax
import jax.numpy as jnp
from jax import lax
from jax.experimental import pallas as pl
from jax.experimental.pallas import tpu as pltpu
from jax.sharding import PartitionSpec as P

GRID_CHIPS = 8
HALVES = 2
BEHIND = (0, 0, 0, 0, 2, 4, 6)


def ring_chip(at):
    at = at % GRID_CHIPS
    back = 2 * ((GRID_CHIPS - at) % GRID_CHIPS)
    up = 2 * at - 1
    if isinstance(at, int):
        return up if 1 <= at <= GRID_CHIPS // 2 else back
    return jnp.where((at >= 1) & (at <= GRID_CHIPS // 2), up, back)


def ring_place(chip):
    z, y = chip // 2, chip % 2
    return jnp.where(y == 1, 1 + z, (GRID_CHIPS - z) % GRID_CHIPS)


def routing(owners, count, slots, block_rows):
    blocks_here = owners.shape[0]
    rows = blocks_here * block_rows
    owner_col = owners[:, 0]
    same = owner_col[:, None] == owner_col[None, :]
    lower = jnp.arange(blocks_here)[:, None] > jnp.arange(blocks_here)[None, :]
    rank = jnp.sum((same & lower).astype(jnp.int32), axis=1)
    target = owner_col * slots + rank
    select = jnp.arange(count * slots, dtype=jnp.int32)[:, None] == target[None, :]
    global_ids = lax.axis_index("wide") * blocks_here + jnp.arange(blocks_here, dtype=jnp.int32)
    labels = jnp.sum(jnp.where(select, global_ids[None, :] + 1, 0), axis=1) - 1
    row_at = jnp.arange(rows, dtype=jnp.int32)
    out_at = jnp.arange(count * block_rows * slots, dtype=jnp.int32)
    row_key = jnp.repeat(target, block_rows) * block_rows + row_at % block_rows
    out_key = (
        out_at // (block_rows * slots) * slots + out_at % slots
    ) * block_rows + out_at // slots % block_rows
    place = (out_key[:, None] == row_key[None, :]).astype(jnp.bfloat16)
    return labels.reshape(count, slots), place


def finish_kernel(place_ref, *refs):
    out_ref = refs[-1]
    mine, theirs = refs[: len(refs) // 2], refs[len(refs) // 2 : -1]
    count, planes, slots, naux = out_ref.shape
    norb = len(mine) // HALVES
    width = naux // HALVES
    for at in range(norb * HALVES):
        i, j = at // HALVES, at % HALVES
        back = (mine[at][...] + theirs[at][...]).astype(jnp.bfloat16)
        out = jnp.dot(place_ref[...], back, preferred_element_type=jnp.float32)
        out = out.astype(jnp.bfloat16).reshape(count, planes // norb, slots, width)
        out_ref[:, pl.ds(i * (planes // norb), planes // norb), :, pl.ds(j * width, width)] = out


def finish(place, mine, theirs, shape):
    return pl.pallas_call(
        finish_kernel,
        out_shape=jax.ShapeDtypeStruct(shape, jnp.bfloat16),
        in_specs=[pl.BlockSpec(memory_space=pltpu.VMEM)] * (1 + len(mine) + len(theirs)),
        out_specs=pl.BlockSpec(memory_space=pltpu.VMEM),
        compiler_params=pltpu.CompilerParams(vmem_limit_bytes=20 << 20),
        cost_estimate=pl.CostEstimate(
            flops=2 * math.prod(shape) * place.shape[1],
            bytes_accessed=2 * math.prod(shape),
            transcendentals=0,
        ),
    )(place, *mine, *theirs)


def spread_kernel(core_ref, c_ref, kept_ref, given_ref):
    chips, _, depth = kept_ref.shape
    second = core_ref[0] == 1
    for chip in range(chips):
        even = c_ref[:, 2 * chip * depth : (2 * chip + 1) * depth]
        odd = c_ref[:, (2 * chip + 1) * depth : (2 * chip + 2) * depth]
        kept_ref[chip] = jnp.where(second, odd, even)
        given_ref[chip] = jnp.where(second, even, odd)


def spread(coefficients, core):
    rows, nvirt = coefficients.shape
    depth = nvirt // (2 * GRID_CHIPS)
    step = 48
    part = pl.BlockSpec((GRID_CHIPS, step, depth), lambda at: (0, at, 0))
    shape = jax.ShapeDtypeStruct((GRID_CHIPS, rows, depth), coefficients.dtype)
    return pl.pallas_call(
        spread_kernel,
        grid=(rows // step,),
        out_shape=(shape, shape),
        in_specs=[
            pl.BlockSpec(memory_space=pltpu.SMEM),
            pl.BlockSpec((step, nvirt), lambda at: (at, 0)),
        ],
        out_specs=(part, part),
        compiler_params=pltpu.CompilerParams(vmem_limit_bytes=16 << 20),
        cost_estimate=pl.CostEstimate(
            flops=0, bytes_accessed=4 * rows * nvirt, transcendentals=0
        ),
    )(core, coefficients)


def after(value, event):
    return lax.optimization_barrier((value, event))[0]


def ring_products(gamma, coefficients):
    count = lax.axis_size("wide")
    rows = coefficients.shape[0]
    norb, depth, naux = gamma.shape
    width = naux // HALVES
    me = lax.axis_index("wide")
    core = me % 2
    here = ring_place(me // 2)
    swap = [(d, d ^ 1) for d in range(count)]

    ways = (1, -1)
    streams = [(i, j) for i in range(norb) for j in range(HALVES)]
    piece = {(i, j): gamma[i, :, j * width : (j + 1) * width] for i, j in streams}
    shift = [
        [
            (2 * ring_chip(p) + k, 2 * ring_chip(p + way) + k)
            for p in range(GRID_CHIPS)
            for k in range(2)
        ]
        for way in ways
    ]
    mine = {s: jnp.zeros((rows, width), jnp.float32) for s in streams}
    theirs = {s: [jnp.zeros((rows, width), jnp.float32)] for s in streams}
    for t in range(GRID_CHIPS):
        arrived = dict(piece)
        if t + 1 < GRID_CHIPS:
            for s in streams:
                done = BEHIND[t]
                sent = after(piece[s], theirs[s][done]) if done else piece[s]
                piece[s] = lax.ppermute(sent, "wide", shift[s[0]])
        if t == 0:
            ready = after(coefficients, piece[streams[-1]])
            kept, given = spread(ready, core.reshape(1))
            taken = lax.ppermute(given, "wide", swap)
        for i, j in streams:
            chip = ring_chip(here - t * ways[i] + GRID_CHIPS)
            block = arrived[i, j]
            left = lax.dynamic_index_in_dim(taken, chip, 0, False)
            term = jnp.dot(left, block, preferred_element_type=jnp.float32)
            theirs[i, j].append(theirs[i, j][-1] + term)
            left = lax.dynamic_index_in_dim(kept, chip, 0, False)
            mine[i, j] += jnp.dot(left, block, preferred_element_type=jnp.float32)
        if t == 2:
            second = arrived[streams[0]]
    swapped = [lax.ppermute(theirs[s][-1], "wide", swap) for s in streams]
    return [mine[s] for s in streams], swapped, second


def local(gamma, coefficients, owners):
    count = lax.axis_size("wide")
    blocks_here = owners.shape[0]
    slots = max(2, 2 * blocks_here // count)
    block_rows = coefficients.shape[0] // blocks_here
    norb, depth, naux = gamma.shape
    shape = (count, norb * block_rows, slots, naux)

    labels, place = routing(owners, count, slots, block_rows)
    if count == 2 * GRID_CHIPS and norb == 2:
        mine, theirs, second = ring_products(gamma, coefficients)
        labels = after(labels, second)
        out = finish(place, mine, theirs, shape)
    else:
        gathered = lax.all_gather(gamma, "wide", axis=1, tiled=True)
        back = jnp.einsum(
            "ra,ian->irn", coefficients, gathered, preferred_element_type=jnp.float32
        ).astype(jnp.bfloat16)
        out = jnp.einsum("tr,irn->itn", place, back, preferred_element_type=jnp.float32)
        out = out.astype(jnp.bfloat16).reshape(norb, count, block_rows, slots, naux)
        out = out.transpose(1, 0, 2, 3, 4).reshape(shape)
    ids = lax.all_to_all(labels, "wide", split_axis=0, concat_axis=0, tiled=True)
    placed = lax.all_to_all(out, "wide", split_axis=0, concat_axis=0, tiled=True)
    return placed.transpose(0, 2, 1, 3)[None], ids[None]


def solution(mesh):
    placed = (P("groups", "wide", None), P("wide", None), P("wide", None))
    return jax.shard_map(
        local,
        mesh=mesh,
        in_specs=placed,
        out_specs=(P("wide", None, "groups", None, None), P("wide", "groups", None)),
        check_vma=False,
    )
```

```python
import functools
import math

import jax
import jax.numpy as jnp
from jax import lax
from jax.experimental import pallas as pl
from jax.experimental.pallas import tpu as pltpu
from jax.sharding import PartitionSpec as P

GRID_CHIPS = 8
HALVES = 2
WAYS = (1, -1)
LANES = 128
WINDOW = 896


def ring_chip(at):
    at = at % GRID_CHIPS
    back = 2 * ((GRID_CHIPS - at) % GRID_CHIPS)
    up = 2 * at - 1
    if isinstance(at, int):
        return up if 1 <= at <= GRID_CHIPS // 2 else back
    return jnp.where((at >= 1) & (at <= GRID_CHIPS // 2), up, back)


def ring_place(chip):
    z, y = chip // 2, chip % 2
    return jnp.where(y == 1, 1 + z, (GRID_CHIPS - z) % GRID_CHIPS)


def routing(owners, count, slots, block_rows):
    blocks_here = owners.shape[0]
    rows = blocks_here * block_rows
    owner_col = owners[:, 0]
    same = owner_col[:, None] == owner_col[None, :]
    lower = jnp.arange(blocks_here)[:, None] > jnp.arange(blocks_here)[None, :]
    rank = jnp.sum((same & lower).astype(jnp.int32), axis=1)
    target = owner_col * slots + rank
    select = jnp.arange(count * slots, dtype=jnp.int32)[:, None] == target[None, :]
    global_ids = lax.axis_index("wide") * blocks_here + jnp.arange(blocks_here, dtype=jnp.int32)
    labels = jnp.sum(jnp.where(select, global_ids[None, :] + 1, 0), axis=1) - 1
    row_at = jnp.arange(rows, dtype=jnp.int32)
    out_at = jnp.arange(count * block_rows * slots, dtype=jnp.int32)
    row_key = jnp.repeat(target, block_rows) * block_rows + row_at % block_rows
    out_key = (
        out_at // (block_rows * slots) * slots + out_at % slots
    ) * block_rows + out_at // slots % block_rows
    place = (out_key[:, None] == row_key[None, :]).astype(jnp.bfloat16)
    return labels.reshape(count, slots), place


def window_at(start, nvirt):
    return jnp.minimum(start // LANES * LANES, nvirt - WINDOW)


def step_kernel(t, own_hbm, other_hbm, *refs):
    norb = len(WAYS)
    pieces = refs[:norb]
    before, (mine_ref, theirs_ref, c_buf, g_buf, sems) = refs[norb:-5], refs[-5:]
    rows, nvirt = own_hbm.shape
    depth = pieces[0].shape[0]
    me = lax.axis_index("wide")
    core = lax.rem(me, 2)
    here = ring_place(lax.div(me, 2))
    shifts, copies = [], []
    for i in range(norb):
        chip = ring_chip(here - t * WAYS[i] + GRID_CHIPS)
        start = (2 * chip + core) * depth
        at = pl.multiple_of(window_at(start, nvirt), LANES)
        shifts.append(pl.multiple_of(start - at, 16))
        columns = pl.ds(at, WINDOW)
        copies.append(
            [
                pltpu.make_async_copy(
                    source.at[:, columns], c_buf.at[i, pl.ds(k * rows, rows)], sems.at[i, k]
                )
                for k, source in enumerate((own_hbm, other_hbm))
            ]
        )
        for copy in copies[i]:
            copy.start()
    for i in range(norb):
        g_buf[i] = jnp.zeros_like(g_buf[i])
        g_buf[i, pl.ds(shifts[i], depth), :] = pieces[i][...]
    for i in range(norb):
        for copy in copies[i]:
            copy.wait()
        term = jnp.dot(c_buf[i], g_buf[i], preferred_element_type=jnp.float32)
        if before:
            mine_ref[i] = before[0][i] + term[:rows]
            theirs_ref[i] = before[1][i] + term[rows:]
        else:
            mine_ref[i] = term[:rows]
            theirs_ref[i] = term[rows:]


def add_products(t, own, other, pieces, before):
    rows, nvirt = own.shape
    norb = len(pieces)
    depth, width = pieces[0].shape
    sums = jax.ShapeDtypeStruct((norb, rows, width), jnp.float32)
    vmem = pl.BlockSpec(memory_space=pltpu.VMEM)
    hbm = pl.BlockSpec(memory_space=pltpu.HBM)
    return pl.pallas_call(
        functools.partial(step_kernel, t),
        out_shape=(sums, sums),
        in_specs=[hbm, hbm] + [vmem] * (norb + len(before)),
        out_specs=(vmem, vmem),
        input_output_aliases={2 + norb + k: k for k in range(len(before))},
        scratch_shapes=[
            pltpu.VMEM((norb, 2 * rows, WINDOW), jnp.bfloat16),
            pltpu.VMEM((norb, WINDOW, width), jnp.bfloat16),
            pltpu.SemaphoreType.DMA((norb, 2)),
        ],
        compiler_params=pltpu.CompilerParams(vmem_limit_bytes=16 << 20),
        cost_estimate=pl.CostEstimate(
            flops=4 * norb * rows * WINDOW * width,
            bytes_accessed=4 * norb * rows * WINDOW,
            transcendentals=0,
        ),
    )(own, other, *pieces, *before)


def finish_kernel(place_ref, *refs):
    out_ref = refs[-1]
    mine, theirs = refs[:HALVES], refs[HALVES:-1]
    count, planes, slots, naux = out_ref.shape
    norb, _, width = mine[0].shape
    for i in range(norb):
        for j in range(HALVES):
            back = (mine[j][i] + theirs[j][i]).astype(jnp.bfloat16)
            out = jnp.dot(place_ref[...], back, preferred_element_type=jnp.float32)
            out = out.astype(jnp.bfloat16).reshape(count, planes // norb, slots, width)
            out_ref[
                :, pl.ds(i * (planes // norb), planes // norb), :, pl.ds(j * width, width)
            ] = out


def finish(place, mine, theirs, shape):
    return pl.pallas_call(
        finish_kernel,
        out_shape=jax.ShapeDtypeStruct(shape, jnp.bfloat16),
        in_specs=[pl.BlockSpec(memory_space=pltpu.VMEM)] * (1 + len(mine) + len(theirs)),
        out_specs=pl.BlockSpec(memory_space=pltpu.VMEM),
        compiler_params=pltpu.CompilerParams(vmem_limit_bytes=20 << 20),
        cost_estimate=pl.CostEstimate(
            flops=2 * math.prod(shape) * place.shape[1],
            bytes_accessed=2 * math.prod(shape),
            transcendentals=0,
        ),
    )(place, *mine, *theirs)


def ring_products(gamma, coefficients, early):
    count = lax.axis_size("wide")
    norb, depth, naux = gamma.shape
    width = naux // HALVES
    swap = [(d, d ^ 1) for d in range(count)]
    other = lax.ppermute(coefficients, "wide", swap)

    piece = [
        [gamma[i, :, j * width : (j + 1) * width] for i in range(norb)] for j in range(HALVES)
    ]
    shift = [
        [
            (2 * ring_chip(p) + k, 2 * ring_chip(p + way) + k)
            for p in range(GRID_CHIPS)
            for k in range(2)
        ]
        for way in WAYS
    ]
    sums = [()] * HALVES
    for t in range(GRID_CHIPS):
        for j in range(HALVES):
            arrived = list(piece[j])
            if t + 1 < GRID_CHIPS:
                for i in range(norb):
                    sent = arrived[i]
                    if t == 2 and i == j == 0:
                        sent, early = lax.optimization_barrier((sent, early))
                    if t >= 4:
                        sent, sums[j] = lax.optimization_barrier((sent, sums[j]))
                    piece[j][i] = lax.ppermute(sent, "wide", shift[i])
            sums[j] = add_products(t, coefficients, other, arrived, sums[j])
    mine = [sums[j][0] for j in range(HALVES)]
    theirs = [lax.ppermute(sums[j][1], "wide", swap) for j in range(HALVES)]
    return mine, theirs, early


def local(gamma, coefficients, owners):
    count = lax.axis_size("wide")
    blocks_here = owners.shape[0]
    slots = max(2, 2 * blocks_here // count)
    block_rows = coefficients.shape[0] // blocks_here
    norb, depth, naux = gamma.shape
    shape = (count, norb * block_rows, slots, naux)

    labels, place = routing(owners, count, slots, block_rows)
    ids = lax.all_to_all(labels, "wide", split_axis=0, concat_axis=0, tiled=True)
    if count == 2 * GRID_CHIPS and norb == len(WAYS):
        mine, theirs, (ids, place) = ring_products(gamma, coefficients, (ids, place))
        out = finish(place, mine, theirs, shape)
    else:
        gathered = lax.all_gather(gamma, "wide", axis=1, tiled=True)
        back = jnp.einsum(
            "ra,ian->irn", coefficients, gathered, preferred_element_type=jnp.float32
        ).astype(jnp.bfloat16)
        out = jnp.einsum("tr,irn->itn", place, back, preferred_element_type=jnp.float32)
        out = out.astype(jnp.bfloat16).reshape(norb, count, block_rows, slots, naux)
        out = out.transpose(1, 0, 2, 3, 4).reshape(shape)
    placed = lax.all_to_all(out, "wide", split_axis=0, concat_axis=0, tiled=True)
    return placed.transpose(0, 2, 1, 3)[None], ids[None]


def solution(mesh):
    placed = (P("groups", "wide", None), P("wide", None), P("wide", None))
    return jax.shard_map(
        local,
        mesh=mesh,
        in_specs=placed,
        out_specs=(P("wide", None, "groups", None, None), P("wide", "groups", None)),
        check_vma=False,
    )
```

```python
import functools
import math

import jax
import jax.numpy as jnp
from jax import lax
from jax.experimental import pallas as pl
from jax.experimental.pallas import tpu as pltpu
from jax.sharding import PartitionSpec as P

GRID_CHIPS = 8
HALVES = 2
BEHIND = (0, 0, 1, 2, 4, 5, 6)
WAYS = (1, -1)
LANES = 128
WINDOW = 896


def ring_chip(at):
    at = at % GRID_CHIPS
    back = 2 * ((GRID_CHIPS - at) % GRID_CHIPS)
    up = 2 * at - 1
    if isinstance(at, int):
        return up if 1 <= at <= GRID_CHIPS // 2 else back
    return jnp.where((at >= 1) & (at <= GRID_CHIPS // 2), up, back)


def ring_place(chip):
    z, y = chip // 2, chip % 2
    return jnp.where(y == 1, 1 + z, (GRID_CHIPS - z) % GRID_CHIPS)


def routing(owners, count, slots, block_rows):
    blocks_here = owners.shape[0]
    rows = blocks_here * block_rows
    owner_col = owners[:, 0]
    same = owner_col[:, None] == owner_col[None, :]
    lower = jnp.arange(blocks_here)[:, None] > jnp.arange(blocks_here)[None, :]
    rank = jnp.sum((same & lower).astype(jnp.int32), axis=1)
    target = owner_col * slots + rank
    select = jnp.arange(count * slots, dtype=jnp.int32)[:, None] == target[None, :]
    global_ids = lax.axis_index("wide") * blocks_here + jnp.arange(blocks_here, dtype=jnp.int32)
    labels = jnp.sum(jnp.where(select, global_ids[None, :] + 1, 0), axis=1) - 1
    row_at = jnp.arange(rows, dtype=jnp.int32)
    out_at = jnp.arange(count * block_rows * slots, dtype=jnp.int32)
    row_key = jnp.repeat(target, block_rows) * block_rows + row_at % block_rows
    out_key = (
        out_at // (block_rows * slots) * slots + out_at % slots
    ) * block_rows + out_at // slots % block_rows
    place = (out_key[:, None] == row_key[None, :]).astype(jnp.bfloat16)
    return labels.reshape(count, slots), place


def window_at(start, nvirt):
    return jnp.minimum(start // LANES * LANES, nvirt - WINDOW)


def step_kernel(t, parts, own_hbm, other_hbm, *refs):
    norb = len(WAYS)
    pieces = refs[: norb * parts]
    scratch = refs[-3:]
    sums = refs[-3 - 2 * parts : -3]
    before = refs[norb * parts : -3 - 2 * parts]
    c_buf, g_buf, sems = scratch
    rows, nvirt = own_hbm.shape
    depth, width = pieces[0].shape
    me = lax.axis_index("wide")
    core = lax.rem(me, 2)
    here = ring_place(lax.div(me, 2))
    shifts, copies = [], []
    for i in range(norb):
        chip = ring_chip(here - t * WAYS[i] + GRID_CHIPS)
        start = (2 * chip + core) * depth
        at = pl.multiple_of(window_at(start, nvirt), LANES)
        shifts.append(pl.multiple_of(start - at, 16))
        columns = pl.ds(at, WINDOW)
        copies.append(
            [
                pltpu.make_async_copy(
                    source.at[:, columns], c_buf.at[i, pl.ds(k * rows, rows)], sems.at[i, k]
                )
                for k, source in enumerate((own_hbm, other_hbm))
            ]
        )
        for copy in copies[i]:
            copy.start()
    for i in range(norb):
        g_buf[i] = jnp.zeros_like(g_buf[i])
        for j in range(parts):
            g_buf[i, pl.ds(shifts[i], depth), pl.ds(j * width, width)] = pieces[
                j * norb + i
            ][...]
    for i in range(norb):
        for copy in copies[i]:
            copy.wait()
        for k in range(2):
            term = jnp.dot(
                c_buf[i, pl.ds(k * rows, rows)], g_buf[i], preferred_element_type=jnp.float32
            )
            for j in range(parts):
                part = term[:, j * width : (j + 1) * width]
                at = 2 * j + k
                sums[at][i] = before[at][i] + part if before else part


def add_products(t, own, other, pieces, before):
    rows, nvirt = own.shape
    parts, norb = len(pieces), len(WAYS)
    depth, width = pieces[0][0].shape
    sums = jax.ShapeDtypeStruct((norb, rows, width), jnp.float32)
    vmem = pl.BlockSpec(memory_space=pltpu.VMEM)
    hbm = pl.BlockSpec(memory_space=pltpu.HBM)
    flat = [piece for part in pieces for piece in part]
    old = [value for pair in before for value in pair]
    new = pl.pallas_call(
        functools.partial(step_kernel, t, parts),
        out_shape=[sums] * (2 * parts),
        in_specs=[hbm, hbm] + [vmem] * (len(flat) + len(old)),
        out_specs=[vmem] * (2 * parts),
        input_output_aliases={2 + len(flat) + k: k for k in range(len(old))},
        scratch_shapes=[
            pltpu.VMEM((norb, 2 * rows, WINDOW), jnp.bfloat16),
            pltpu.VMEM((norb, WINDOW, parts * width), jnp.bfloat16),
            pltpu.SemaphoreType.DMA((norb, 2)),
        ],
        compiler_params=pltpu.CompilerParams(vmem_limit_bytes=20 << 20),
        cost_estimate=pl.CostEstimate(
            flops=4 * norb * rows * WINDOW * parts * width,
            bytes_accessed=4 * norb * rows * WINDOW,
            transcendentals=0,
        ),
    )(own, other, *flat, *old)
    return [(new[2 * j], new[2 * j + 1]) for j in range(parts)]


def finish_kernel(place_ref, *refs):
    out_ref = refs[-1]
    mine, theirs = refs[:HALVES], refs[HALVES:-1]
    count, planes, slots, naux = out_ref.shape
    norb, _, width = mine[0].shape
    for i in range(norb):
        for j in range(HALVES):
            back = (mine[j][i] + theirs[j][i]).astype(jnp.bfloat16)
            out = jnp.dot(place_ref[...], back, preferred_element_type=jnp.float32)
            out = out.astype(jnp.bfloat16).reshape(count, planes // norb, slots, width)
            out_ref[
                :, pl.ds(i * (planes // norb), planes // norb), :, pl.ds(j * width, width)
            ] = out


def finish(place, mine, theirs, shape):
    return pl.pallas_call(
        finish_kernel,
        out_shape=jax.ShapeDtypeStruct(shape, jnp.bfloat16),
        in_specs=[pl.BlockSpec(memory_space=pltpu.VMEM)] * (1 + len(mine) + len(theirs)),
        out_specs=pl.BlockSpec(memory_space=pltpu.VMEM),
        compiler_params=pltpu.CompilerParams(vmem_limit_bytes=20 << 20),
        cost_estimate=pl.CostEstimate(
            flops=2 * math.prod(shape) * place.shape[1],
            bytes_accessed=2 * math.prod(shape),
            transcendentals=0,
        ),
    )(place, *mine, *theirs)


def ring_products(gamma, coefficients, early):
    count = lax.axis_size("wide")
    norb, depth, naux = gamma.shape
    width = naux // HALVES
    swap = [(d, d ^ 1) for d in range(count)]
    other = lax.ppermute(coefficients, "wide", swap)

    piece = [
        [gamma[i, :, j * width : (j + 1) * width] for i in range(norb)] for j in range(HALVES)
    ]
    shift = [
        [
            (2 * ring_chip(p) + k, 2 * ring_chip(p + way) + k)
            for p in range(GRID_CHIPS)
            for k in range(2)
        ]
        for way in WAYS
    ]
    arrived, sums, done = [], [], 0
    for t in range(GRID_CHIPS):
        arrived.append([list(part) for part in piece])
        if t + 1 == GRID_CHIPS:
            break
        for j in range(HALVES):
            if j == HALVES - 1:
                while done < BEHIND[t]:
                    sums = add_products(done, coefficients, other, arrived[done], sums)
                    done += 1
            for i in range(norb):
                sent = piece[j][i]
                if t == 2 and i == j == 0:
                    sent, early = lax.optimization_barrier((sent, early))
                if j == HALVES - 1 and BEHIND[t]:
                    sent, sums = lax.optimization_barrier((sent, sums))
                piece[j][i] = lax.ppermute(sent, "wide", shift[i])
    while done < GRID_CHIPS - 1:
        sums = add_products(done, coefficients, other, arrived[done], sums)
        done += 1
    sums = [
        add_products(done, coefficients, other, [arrived[done][j]], [sums[j]])[0]
        for j in range(HALVES)
    ]
    mine = [sums[j][0] for j in range(HALVES)]
    theirs = [lax.ppermute(sums[j][1], "wide", swap) for j in range(HALVES)]
    return mine, theirs, early


def local(gamma, coefficients, owners):
    count = lax.axis_size("wide")
    blocks_here = owners.shape[0]
    slots = max(2, 2 * blocks_here // count)
    block_rows = coefficients.shape[0] // blocks_here
    norb, depth, naux = gamma.shape
    shape = (count, norb * block_rows, slots, naux)

    labels, place = routing(owners, count, slots, block_rows)
    ids = lax.all_to_all(labels, "wide", split_axis=0, concat_axis=0, tiled=True)
    if count == 2 * GRID_CHIPS and norb == len(WAYS):
        mine, theirs, (ids, place) = ring_products(gamma, coefficients, (ids, place))
        out = finish(place, mine, theirs, shape)
    else:
        gathered = lax.all_gather(gamma, "wide", axis=1, tiled=True)
        back = jnp.einsum(
            "ra,ian->irn", coefficients, gathered, preferred_element_type=jnp.float32
        ).astype(jnp.bfloat16)
        out = jnp.einsum("tr,irn->itn", place, back, preferred_element_type=jnp.float32)
        out = out.astype(jnp.bfloat16).reshape(norb, count, block_rows, slots, naux)
        out = out.transpose(1, 0, 2, 3, 4).reshape(shape)
    placed = lax.all_to_all(out, "wide", split_axis=0, concat_axis=0, tiled=True)
    return placed.transpose(0, 2, 1, 3)[None], ids[None]


def solution(mesh):
    placed = (P("groups", "wide", None), P("wide", None), P("wide", None))
    return jax.shard_map(
        local,
        mesh=mesh,
        in_specs=placed,
        out_specs=(P("wide", None, "groups", None, None), P("wide", "groups", None)),
        check_vma=False,
    )
```

```python
import functools
import math

import jax
import jax.numpy as jnp
from jax import lax
from jax.experimental import pallas as pl
from jax.experimental.pallas import tpu as pltpu
from jax.sharding import PartitionSpec as P

GRID_CHIPS = 8
HALVES = 2
BEHIND = (0, 0, 0, 2, 3, 4, 5)
WAYS = (1, -1)
LANES = 128
WINDOW = 896


def ring_chip(at):
    at = at % GRID_CHIPS
    back = 2 * ((GRID_CHIPS - at) % GRID_CHIPS)
    up = 2 * at - 1
    if isinstance(at, int):
        return up if 1 <= at <= GRID_CHIPS // 2 else back
    return jnp.where((at >= 1) & (at <= GRID_CHIPS // 2), up, back)


def ring_place(chip):
    z, y = chip // 2, chip % 2
    return jnp.where(y == 1, 1 + z, (GRID_CHIPS - z) % GRID_CHIPS)


def routing(owners, count, slots, block_rows):
    blocks_here = owners.shape[0]
    rows = blocks_here * block_rows
    owner_col = owners[:, 0]
    same = owner_col[:, None] == owner_col[None, :]
    lower = jnp.arange(blocks_here)[:, None] > jnp.arange(blocks_here)[None, :]
    rank = jnp.sum((same & lower).astype(jnp.int32), axis=1)
    target = owner_col * slots + rank
    select = jnp.arange(count * slots, dtype=jnp.int32)[:, None] == target[None, :]
    global_ids = lax.axis_index("wide") * blocks_here + jnp.arange(blocks_here, dtype=jnp.int32)
    labels = jnp.sum(jnp.where(select, global_ids[None, :] + 1, 0), axis=1) - 1
    row_at = jnp.arange(rows, dtype=jnp.int32)
    out_at = jnp.arange(count * block_rows * slots, dtype=jnp.int32)
    row_key = jnp.repeat(target, block_rows) * block_rows + row_at % block_rows
    out_key = (
        out_at // (block_rows * slots) * slots + out_at % slots
    ) * block_rows + out_at // slots % block_rows
    place = (out_key[:, None] == row_key[None, :]).astype(jnp.bfloat16)
    return labels.reshape(count, slots), place


def window_at(start, nvirt):
    return jnp.minimum(start // LANES * LANES, nvirt - WINDOW)


def step_kernel(t, parts, sides, own_hbm, other_hbm, *refs):
    norb = len(WAYS)
    pieces = refs[: norb * parts]
    c_buf, g_buf, sems = refs[-3:]
    results = parts * len(sides)
    sums = refs[-3 - results : -3]
    before = refs[norb * parts : -3 - results]
    rows, nvirt = own_hbm.shape
    depth, width = pieces[0].shape
    me = lax.axis_index("wide")
    core = lax.rem(me, 2)
    here = ring_place(lax.div(me, 2))
    shifts, copies = [], []
    for i in range(norb):
        chip = ring_chip(here - t * WAYS[i] + GRID_CHIPS)
        start = (2 * chip + core) * depth
        at = pl.multiple_of(window_at(start, nvirt), LANES)
        shifts.append(pl.multiple_of(start - at, 16))
        columns = pl.ds(at, WINDOW)
        copies.append(
            [
                pltpu.make_async_copy(
                    (own_hbm, other_hbm)[side].at[:, columns],
                    c_buf.at[i, pl.ds(k * rows, rows)],
                    sems.at[i, k],
                )
                for k, side in enumerate(sides)
            ]
        )
        for copy in copies[i]:
            copy.start()
    for i in range(norb):
        g_buf[i] = jnp.zeros_like(g_buf[i])
        for j in range(parts):
            g_buf[i, pl.ds(shifts[i], depth), pl.ds(j * width, width)] = pieces[
                j * norb + i
            ][...]
    for i in range(norb):
        for copy in copies[i]:
            copy.wait()
        for k in range(len(sides)):
            term = jnp.dot(
                c_buf[i, pl.ds(k * rows, rows)], g_buf[i], preferred_element_type=jnp.float32
            )
            for j in range(parts):
                part = term[:, j * width : (j + 1) * width]
                at = len(sides) * j + k
                sums[at][i] = before[at][i] + part if before else part


def add_products(t, own, other, pieces, before, sides=(0, 1)):
    rows, nvirt = own.shape
    parts, norb = len(pieces), len(WAYS)
    depth, width = pieces[0][0].shape
    sums = jax.ShapeDtypeStruct((norb, rows, width), jnp.float32)
    vmem = pl.BlockSpec(memory_space=pltpu.VMEM)
    hbm = pl.BlockSpec(memory_space=pltpu.HBM)
    flat = [piece for part in pieces for piece in part]
    old = [value for some in before for value in some]
    results = parts * len(sides)
    new = pl.pallas_call(
        functools.partial(step_kernel, t, parts, sides),
        out_shape=[sums] * results,
        in_specs=[hbm, hbm] + [vmem] * (len(flat) + len(old)),
        out_specs=[vmem] * results,
        input_output_aliases={2 + len(flat) + k: k for k in range(len(old))},
        scratch_shapes=[
            pltpu.VMEM((norb, len(sides) * rows, WINDOW), jnp.bfloat16),
            pltpu.VMEM((norb, WINDOW, parts * width), jnp.bfloat16),
            pltpu.SemaphoreType.DMA((norb, len(sides))),
        ],
        compiler_params=pltpu.CompilerParams(vmem_limit_bytes=20 << 20),
        cost_estimate=pl.CostEstimate(
            flops=2 * len(sides) * norb * rows * WINDOW * parts * width,
            bytes_accessed=2 * len(sides) * norb * rows * WINDOW,
            transcendentals=0,
        ),
    )(own, other, *flat, *old)
    return [tuple(new[len(sides) * j : len(sides) * (j + 1)]) for j in range(parts)]


def finish_kernel(place_ref, mine_ref, theirs_ref, *refs):
    out_ref = refs[-1]
    norb, _, width = mine_ref.shape
    count, planes, slots, naux = out_ref.shape
    for before in refs[:-1]:
        out_ref[:, :, :, : naux - width] = before[...]
    for i in range(norb):
        back = (mine_ref[i] + theirs_ref[i]).astype(jnp.bfloat16)
        out = jnp.dot(place_ref[...], back, preferred_element_type=jnp.float32)
        out = out.astype(jnp.bfloat16).reshape(count, planes // norb, slots, width)
        plane = pl.ds(i * (planes // norb), planes // norb)
        out_ref[:, plane, :, pl.ds(naux - width, width)] = out


def finish(place, mine, theirs, before, shape):
    vmem = pl.BlockSpec(memory_space=pltpu.VMEM)
    return pl.pallas_call(
        finish_kernel,
        out_shape=jax.ShapeDtypeStruct(shape, jnp.bfloat16),
        in_specs=[vmem] * (3 + len(before)),
        out_specs=vmem,
        compiler_params=pltpu.CompilerParams(vmem_limit_bytes=20 << 20),
        cost_estimate=pl.CostEstimate(
            flops=2 * math.prod(shape) * place.shape[1],
            bytes_accessed=2 * math.prod(shape),
            transcendentals=0,
        ),
    )(place, mine, theirs, *before)


def ring_products(gamma, coefficients, ids, place, shape):
    count = lax.axis_size("wide")
    norb, depth, naux = gamma.shape
    width = naux // HALVES
    swap = [(d, d ^ 1) for d in range(count)]
    other = lax.ppermute(coefficients, "wide", swap)

    piece = [
        [gamma[i, :, j * width : (j + 1) * width] for i in range(norb)] for j in range(HALVES)
    ]
    shift = [
        [
            (2 * ring_chip(p) + k, 2 * ring_chip(p + way) + k)
            for p in range(GRID_CHIPS)
            for k in range(2)
        ]
        for way in WAYS
    ]
    arrived, sums, done = [], [], 0
    for t in range(GRID_CHIPS):
        arrived.append([list(part) for part in piece])
        if t + 1 == GRID_CHIPS:
            break
        for j in range(HALVES):
            if j == 0:
                while done < BEHIND[t]:
                    sums = add_products(done, coefficients, other, arrived[done], sums)
                    done += 1
            for i in range(norb):
                sent = piece[j][i]
                if t == 2 and i == j == 0:
                    sent, ids, place = lax.optimization_barrier((sent, ids, place))
                if j == 0 and BEHIND[t]:
                    sent, sums = lax.optimization_barrier((sent, sums))
                piece[j][i] = lax.ppermute(sent, "wide", shift[i])
    while done < GRID_CHIPS - 1:
        sums = add_products(done, coefficients, other, arrived[done], sums)
        done += 1
    out = []
    for j in range(HALVES):
        last, out = lax.optimization_barrier(([arrived[done][j]], out))
        mine, theirs = sums[j]
        ((theirs,),) = add_products(done, coefficients, other, last, [(theirs,)], (1,))
        theirs = lax.ppermute(theirs, "wide", swap)
        ((mine,),) = add_products(done, coefficients, other, last, [(mine,)], (0,))
        out = [finish(place, mine, theirs, out, shape[:3] + ((j + 1) * width,))]
    return ids, out[0]


def local(gamma, coefficients, owners):
    count = lax.axis_size("wide")
    blocks_here = owners.shape[0]
    slots = max(2, 2 * blocks_here // count)
    block_rows = coefficients.shape[0] // blocks_here
    norb, depth, naux = gamma.shape
    shape = (count, norb * block_rows, slots, naux)

    labels, place = routing(owners, count, slots, block_rows)
    ids = lax.all_to_all(labels, "wide", split_axis=0, concat_axis=0, tiled=True)
    if count == 2 * GRID_CHIPS and norb == len(WAYS):
        ids, out = ring_products(gamma, coefficients, ids, place, shape)
    else:
        gathered = lax.all_gather(gamma, "wide", axis=1, tiled=True)
        back = jnp.einsum(
            "ra,ian->irn", coefficients, gathered, preferred_element_type=jnp.float32
        ).astype(jnp.bfloat16)
        out = jnp.einsum("tr,irn->itn", place, back, preferred_element_type=jnp.float32)
        out = out.astype(jnp.bfloat16).reshape(norb, count, block_rows, slots, naux)
        out = out.transpose(1, 0, 2, 3, 4).reshape(shape)
    placed = lax.all_to_all(out, "wide", split_axis=0, concat_axis=0, tiled=True)
    return placed.transpose(0, 2, 1, 3)[None], ids[None]


def solution(mesh):
    placed = (P("groups", "wide", None), P("wide", None), P("wide", None))
    return jax.shard_map(
        local,
        mesh=mesh,
        in_specs=placed,
        out_specs=(P("wide", None, "groups", None, None), P("wide", "groups", None)),
        check_vma=False,
    )
```

```python
import functools
import math

import jax
import jax.numpy as jnp
from jax import lax
from jax.experimental import pallas as pl
from jax.experimental.pallas import tpu as pltpu
from jax.sharding import PartitionSpec as P

GRID_CHIPS = 8
HALVES = 2
BEHIND = ((0, 0), (0, 0), (0, 1), (1, 2), (2, 4), (4, 5), (5, 6))
WAYS = (1, -1)
LANES = 128
WINDOW = 896


def ring_chip(at):
    at = at % GRID_CHIPS
    back = 2 * ((GRID_CHIPS - at) % GRID_CHIPS)
    up = 2 * at - 1
    if isinstance(at, int):
        return up if 1 <= at <= GRID_CHIPS // 2 else back
    return jnp.where((at >= 1) & (at <= GRID_CHIPS // 2), up, back)


def ring_place(chip):
    z, y = chip // 2, chip % 2
    return jnp.where(y == 1, 1 + z, (GRID_CHIPS - z) % GRID_CHIPS)


def routing(owners, count, slots, block_rows):
    blocks_here = owners.shape[0]
    rows = blocks_here * block_rows
    owner_col = owners[:, 0]
    same = owner_col[:, None] == owner_col[None, :]
    lower = jnp.arange(blocks_here)[:, None] > jnp.arange(blocks_here)[None, :]
    rank = jnp.sum((same & lower).astype(jnp.int32), axis=1)
    target = owner_col * slots + rank
    select = jnp.arange(count * slots, dtype=jnp.int32)[:, None] == target[None, :]
    global_ids = lax.axis_index("wide") * blocks_here + jnp.arange(blocks_here, dtype=jnp.int32)
    labels = jnp.sum(jnp.where(select, global_ids[None, :] + 1, 0), axis=1) - 1
    row_at = jnp.arange(rows, dtype=jnp.int32)
    out_at = jnp.arange(count * block_rows * slots, dtype=jnp.int32)
    row_key = jnp.repeat(target, block_rows) * block_rows + row_at % block_rows
    out_key = (
        out_at // (block_rows * slots) * slots + out_at % slots
    ) * block_rows + out_at // slots % block_rows
    place = (out_key[:, None] == row_key[None, :]).astype(jnp.bfloat16)
    return labels.reshape(count, slots), place


def window_at(start, nvirt):
    return jnp.minimum(start // LANES * LANES, nvirt - WINDOW)


def step_kernel(t, parts, own_hbm, other_hbm, *refs):
    norb = len(WAYS)
    pieces = refs[: norb * parts]
    c_buf, g_buf, sems = refs[-3:]
    sums = refs[-3 - 2 * parts : -3]
    before = refs[norb * parts : -3 - 2 * parts]
    rows, nvirt = own_hbm.shape
    depth, width = pieces[0].shape
    me = lax.axis_index("wide")
    core = lax.rem(me, 2)
    here = ring_place(lax.div(me, 2))
    shifts, copies = [], []
    for i in range(norb):
        chip = ring_chip(here - t * WAYS[i] + GRID_CHIPS)
        start = (2 * chip + core) * depth
        at = pl.multiple_of(window_at(start, nvirt), LANES)
        shifts.append(pl.multiple_of(start - at, 16))
        columns = pl.ds(at, WINDOW)
        copies.append(
            [
                pltpu.make_async_copy(
                    source.at[:, columns], c_buf.at[i, pl.ds(k * rows, rows)], sems.at[i, k]
                )
                for k, source in enumerate((own_hbm, other_hbm))
            ]
        )
        for copy in copies[i]:
            copy.start()
    for i in range(norb):
        g_buf[i] = jnp.zeros_like(g_buf[i])
        for j in range(parts):
            g_buf[i, pl.ds(shifts[i], depth), pl.ds(j * width, width)] = pieces[
                j * norb + i
            ][...]
    for i in range(norb):
        for copy in copies[i]:
            copy.wait()
        for k in range(2):
            term = jnp.dot(
                c_buf[i, pl.ds(k * rows, rows)], g_buf[i], preferred_element_type=jnp.float32
            )
            for j in range(parts):
                part = term[:, j * width : (j + 1) * width]
                at = 2 * j + k
                sums[at][i] = before[at][i] + part if before else part


def last_kernel(t, c_ref, *refs):
    norb = len(WAYS)
    pieces, before, sums, g_buf = refs[:norb], refs[norb : norb + 2], refs[-3:-1], refs[-1]
    rows = before[0].shape[1]
    depth = pieces[0].shape[0]
    nvirt = depth * 2 * GRID_CHIPS
    me = lax.axis_index("wide")
    for i in range(norb):
        chip = ring_chip(ring_place(lax.div(me, 2)) - t * WAYS[i] + GRID_CHIPS)
        start = (2 * chip + lax.rem(me, 2)) * depth
        shift = pl.multiple_of(start - window_at(start, nvirt), 16)
        g_buf[i] = jnp.zeros_like(g_buf[i])
        g_buf[i, pl.ds(shift, depth), :] = pieces[i][...]
    for i in range(norb):
        for k in range(2):
            term = jnp.dot(
                c_ref[i, pl.ds(k * rows, rows)], g_buf[i], preferred_element_type=jnp.float32
            )
            sums[k][i] = before[k][i] + term


def add_last_products(t, windows, pieces, before):
    norb = len(WAYS)
    depth, width = pieces[0].shape
    vmem = pl.BlockSpec(memory_space=pltpu.VMEM)
    sums = jax.ShapeDtypeStruct(before[0].shape, jnp.float32)
    return pl.pallas_call(
        functools.partial(last_kernel, t),
        out_shape=[sums] * 2,
        in_specs=[vmem] * (1 + norb + 2),
        out_specs=[vmem] * 2,
        input_output_aliases={1 + norb + k: k for k in range(2)},
        scratch_shapes=[pltpu.VMEM((norb, WINDOW, width), jnp.bfloat16)],
        compiler_params=pltpu.CompilerParams(vmem_limit_bytes=20 << 20),
        cost_estimate=pl.CostEstimate(
            flops=2 * windows.size * width,
            bytes_accessed=2 * windows.size,
            transcendentals=0,
        ),
    )(windows, *pieces, *before)


def add_products(t, own, other, pieces, before, keep=False):
    rows, nvirt = own.shape
    parts, norb = len(pieces), len(WAYS)
    depth, width = pieces[0][0].shape
    sums = jax.ShapeDtypeStruct((norb, rows, width), jnp.float32)
    vmem = pl.BlockSpec(memory_space=pltpu.VMEM)
    hbm = pl.BlockSpec(memory_space=pltpu.HBM)
    flat = [piece for part in pieces for piece in part]
    old = [value for pair in before for value in pair]
    windows = (norb, 2 * rows, WINDOW)
    kept = [jax.ShapeDtypeStruct(windows, own.dtype)] * keep
    new = pl.pallas_call(
        functools.partial(step_kernel, t, parts),
        out_shape=[sums] * (2 * parts) + kept,
        in_specs=[hbm, hbm] + [vmem] * (len(flat) + len(old)),
        out_specs=[vmem] * (2 * parts + keep),
        input_output_aliases={2 + len(flat) + k: k for k in range(len(old))},
        scratch_shapes=[pltpu.VMEM(windows, own.dtype)] * (not keep)
        + [
            pltpu.VMEM((norb, WINDOW, parts * width), jnp.bfloat16),
            pltpu.SemaphoreType.DMA((norb, 2)),
        ],
        compiler_params=pltpu.CompilerParams(vmem_limit_bytes=20 << 20),
        cost_estimate=pl.CostEstimate(
            flops=4 * norb * rows * WINDOW * parts * width,
            bytes_accessed=4 * norb * rows * WINDOW,
            transcendentals=0,
        ),
    )(own, other, *flat, *old)
    pairs = [(new[2 * j], new[2 * j + 1]) for j in range(parts)]
    return (pairs, new[-1]) if keep else pairs


def finish_kernel(place_ref, *refs):
    out_ref = refs[-1]
    mine, theirs = refs[:HALVES], refs[HALVES:-1]
    count, planes, slots, naux = out_ref.shape
    norb, _, width = mine[0].shape
    for i in range(norb):
        for j in range(HALVES):
            back = (mine[j][i] + theirs[j][i]).astype(jnp.bfloat16)
            out = jnp.dot(place_ref[...], back, preferred_element_type=jnp.float32)
            out = out.astype(jnp.bfloat16).reshape(count, planes // norb, slots, width)
            out_ref[
                :, pl.ds(i * (planes // norb), planes // norb), :, pl.ds(j * width, width)
            ] = out


def finish(place, mine, theirs, shape):
    return pl.pallas_call(
        finish_kernel,
        out_shape=jax.ShapeDtypeStruct(shape, jnp.bfloat16),
        in_specs=[pl.BlockSpec(memory_space=pltpu.VMEM)] * (1 + len(mine) + len(theirs)),
        out_specs=pl.BlockSpec(memory_space=pltpu.VMEM),
        compiler_params=pltpu.CompilerParams(vmem_limit_bytes=20 << 20),
        cost_estimate=pl.CostEstimate(
            flops=2 * math.prod(shape) * place.shape[1],
            bytes_accessed=2 * math.prod(shape),
            transcendentals=0,
        ),
    )(place, *mine, *theirs)


def ring_products(gamma, coefficients, early):
    count = lax.axis_size("wide")
    norb, depth, naux = gamma.shape
    width = naux // HALVES
    swap = [(d, d ^ 1) for d in range(count)]
    other = lax.ppermute(coefficients, "wide", swap)

    piece = [
        [gamma[i, :, j * width : (j + 1) * width] for i in range(norb)] for j in range(HALVES)
    ]
    shift = [
        [
            (2 * ring_chip(p) + k, 2 * ring_chip(p + way) + k)
            for p in range(GRID_CHIPS)
            for k in range(2)
        ]
        for way in WAYS
    ]
    arrived, sums, done = [], [], 0
    for t in range(GRID_CHIPS):
        arrived.append([list(part) for part in piece])
        if t + 1 == GRID_CHIPS:
            break
        for j in range(HALVES):
            while done < BEHIND[t][j]:
                sums = add_products(done, coefficients, other, arrived[done], sums)
                done += 1
            for i in range(norb):
                sent = piece[j][i]
                if t == 2 and i == j == 0:
                    sent, early = lax.optimization_barrier((sent, early))
                if BEHIND[t][j]:
                    sent, sums = lax.optimization_barrier((sent, sums))
                piece[j][i] = lax.ppermute(sent, "wide", shift[i])
    while done < GRID_CHIPS - 1:
        sums = add_products(done, coefficients, other, arrived[done], sums)
        done += 1
    sums[:1], windows = add_products(
        done, coefficients, other, arrived[done][:1], sums[:1], keep=True
    )
    sums[1] = add_last_products(done, windows, arrived[done][1], sums[1])
    mine = [sums[j][0] for j in range(HALVES)]
    theirs = [lax.ppermute(sums[j][1], "wide", swap) for j in range(HALVES)]
    return mine, theirs, early


def local(gamma, coefficients, owners):
    count = lax.axis_size("wide")
    blocks_here = owners.shape[0]
    slots = max(2, 2 * blocks_here // count)
    block_rows = coefficients.shape[0] // blocks_here
    norb, depth, naux = gamma.shape
    shape = (count, norb * block_rows, slots, naux)

    labels, place = routing(owners, count, slots, block_rows)
    ids = lax.all_to_all(labels, "wide", split_axis=0, concat_axis=0, tiled=True)
    if count == 2 * GRID_CHIPS and norb == len(WAYS):
        mine, theirs, (ids, place) = ring_products(gamma, coefficients, (ids, place))
        out = finish(place, mine, theirs, shape)
    else:
        gathered = lax.all_gather(gamma, "wide", axis=1, tiled=True)
        back = jnp.einsum(
            "ra,ian->irn", coefficients, gathered, preferred_element_type=jnp.float32
        ).astype(jnp.bfloat16)
        out = jnp.einsum("tr,irn->itn", place, back, preferred_element_type=jnp.float32)
        out = out.astype(jnp.bfloat16).reshape(norb, count, block_rows, slots, naux)
        out = out.transpose(1, 0, 2, 3, 4).reshape(shape)
    placed = lax.all_to_all(out, "wide", split_axis=0, concat_axis=0, tiled=True)
    return placed.transpose(0, 2, 1, 3)[None], ids[None]


def solution(mesh):
    placed = (P("groups", "wide", None), P("wide", None), P("wide", None))
    return jax.shard_map(
        local,
        mesh=mesh,
        in_specs=placed,
        out_specs=(P("wide", None, "groups", None, None), P("wide", "groups", None)),
        check_vma=False,
    )
```

```python
import functools
import math

import jax
import jax.numpy as jnp
from jax import lax
from jax.experimental import pallas as pl
from jax.experimental.pallas import tpu as pltpu
from jax.sharding import PartitionSpec as P

GRID_CHIPS = 8
HALVES = 2
BEHIND = ((0, 0), (0, 0), (0, 1), (1, 2), (2, 4), (4, 5), (5, 6))
WAYS = (1, -1)
LANES = 128
WINDOW = 896


def ring_chip(at):
    at = at % GRID_CHIPS
    back = 2 * ((GRID_CHIPS - at) % GRID_CHIPS)
    up = 2 * at - 1
    if isinstance(at, int):
        return up if 1 <= at <= GRID_CHIPS // 2 else back
    return jnp.where((at >= 1) & (at <= GRID_CHIPS // 2), up, back)


def ring_place(chip):
    z, y = chip // 2, chip % 2
    return jnp.where(y == 1, 1 + z, (GRID_CHIPS - z) % GRID_CHIPS)


def routing(owners, count, slots, block_rows, mask):
    blocks_here = owners.shape[0]
    rows = blocks_here * block_rows
    owner_col = owners[:, 0]
    same = owner_col[:, None] == owner_col[None, :]
    lower = jnp.arange(blocks_here)[:, None] > jnp.arange(blocks_here)[None, :]
    rank = jnp.sum((same & lower).astype(jnp.int32), axis=1)
    target = owner_col * slots + rank
    select = jnp.arange(count * slots, dtype=jnp.int32)[:, None] == target[None, :]
    global_ids = lax.axis_index("wide") * blocks_here + jnp.arange(blocks_here, dtype=jnp.int32)
    labels = jnp.sum(jnp.where(select, global_ids[None, :] + 1, 0), axis=1) - 1
    row_at = jnp.arange(rows, dtype=jnp.int32)
    out_at = jnp.arange(count * block_rows * slots, dtype=jnp.int32)
    row_key = jnp.repeat(target, block_rows) * block_rows + row_at % block_rows
    owner_at = out_at // (block_rows * slots) ^ mask
    out_key = (owner_at * slots + out_at % slots) * block_rows + out_at // slots % block_rows
    place = (out_key[:, None] == row_key[None, :]).astype(jnp.bfloat16)
    return labels.reshape(count, slots), place


def window_at(start, nvirt):
    return jnp.minimum(start // LANES * LANES, nvirt - WINDOW)


def step_kernel(t, parts, own_hbm, other_hbm, *refs):
    norb = len(WAYS)
    pieces = refs[: norb * parts]
    c_buf, g_buf, sems = refs[-3:]
    sums = refs[-3 - 2 * parts : -3]
    before = refs[norb * parts : -3 - 2 * parts]
    rows, nvirt = own_hbm.shape
    depth, width = pieces[0].shape
    me = lax.axis_index("wide")
    core = lax.rem(me, 2)
    here = ring_place(lax.div(me, 2))
    shifts, copies = [], []
    for i in range(norb):
        chip = ring_chip(here - t * WAYS[i] + GRID_CHIPS)
        start = (2 * chip + core) * depth
        at = pl.multiple_of(window_at(start, nvirt), LANES)
        shifts.append(pl.multiple_of(start - at, 16))
        columns = pl.ds(at, WINDOW)
        copies.append(
            [
                pltpu.make_async_copy(
                    source.at[:, columns], c_buf.at[i, pl.ds(k * rows, rows)], sems.at[i, k]
                )
                for k, source in enumerate((own_hbm, other_hbm))
            ]
        )
        for copy in copies[i]:
            copy.start()
    for i in range(norb):
        g_buf[i] = jnp.zeros_like(g_buf[i])
        for j in range(parts):
            g_buf[i, pl.ds(shifts[i], depth), pl.ds(j * width, width)] = pieces[
                j * norb + i
            ][...]
    for i in range(norb):
        for copy in copies[i]:
            copy.wait()
        for k in range(2):
            term = jnp.dot(
                c_buf[i, pl.ds(k * rows, rows)], g_buf[i], preferred_element_type=jnp.float32
            )
            for j in range(parts):
                part = term[:, j * width : (j + 1) * width]
                at = 2 * j + k
                sums[at][i] = before[at][i] + part if before else part


def last_kernel(t, c_ref, *refs):
    norb = len(WAYS)
    pieces, before, sums, g_buf = refs[:norb], refs[norb : norb + 2], refs[-3:-1], refs[-1]
    rows = before[0].shape[1]
    depth = pieces[0].shape[0]
    nvirt = depth * 2 * GRID_CHIPS
    me = lax.axis_index("wide")
    for i in range(norb):
        chip = ring_chip(ring_place(lax.div(me, 2)) - t * WAYS[i] + GRID_CHIPS)
        start = (2 * chip + lax.rem(me, 2)) * depth
        shift = pl.multiple_of(start - window_at(start, nvirt), 16)
        g_buf[i] = jnp.zeros_like(g_buf[i])
        g_buf[i, pl.ds(shift, depth), :] = pieces[i][...]
    for i in range(norb):
        for k in range(2):
            term = jnp.dot(
                c_ref[i, pl.ds(k * rows, rows)], g_buf[i], preferred_element_type=jnp.float32
            )
            sums[k][i] = before[k][i] + term


def add_last_products(t, windows, pieces, before):
    norb = len(WAYS)
    depth, width = pieces[0].shape
    vmem = pl.BlockSpec(memory_space=pltpu.VMEM)
    sums = jax.ShapeDtypeStruct(before[0].shape, jnp.float32)
    return pl.pallas_call(
        functools.partial(last_kernel, t),
        out_shape=[sums] * 2,
        in_specs=[vmem] * (1 + norb + 2),
        out_specs=[vmem] * 2,
        input_output_aliases={1 + norb + k: k for k in range(2)},
        scratch_shapes=[pltpu.VMEM((norb, WINDOW, width), jnp.bfloat16)],
        compiler_params=pltpu.CompilerParams(vmem_limit_bytes=20 << 20),
        cost_estimate=pl.CostEstimate(
            flops=2 * windows.size * width,
            bytes_accessed=2 * windows.size,
            transcendentals=0,
        ),
    )(windows, *pieces, *before)


def add_products(t, own, other, pieces, before, keep=False):
    rows, nvirt = own.shape
    parts, norb = len(pieces), len(WAYS)
    depth, width = pieces[0][0].shape
    sums = jax.ShapeDtypeStruct((norb, rows, width), jnp.float32)
    vmem = pl.BlockSpec(memory_space=pltpu.VMEM)
    hbm = pl.BlockSpec(memory_space=pltpu.HBM)
    flat = [piece for part in pieces for piece in part]
    old = [value for pair in before for value in pair]
    windows = (norb, 2 * rows, WINDOW)
    kept = [jax.ShapeDtypeStruct(windows, own.dtype)] * keep
    new = pl.pallas_call(
        functools.partial(step_kernel, t, parts),
        out_shape=[sums] * (2 * parts) + kept,
        in_specs=[hbm, hbm] + [vmem] * (len(flat) + len(old)),
        out_specs=[vmem] * (2 * parts + keep),
        input_output_aliases={2 + len(flat) + k: k for k in range(len(old))},
        scratch_shapes=[pltpu.VMEM(windows, own.dtype)] * (not keep)
        + [
            pltpu.VMEM((norb, WINDOW, parts * width), jnp.bfloat16),
            pltpu.SemaphoreType.DMA((norb, 2)),
        ],
        compiler_params=pltpu.CompilerParams(vmem_limit_bytes=20 << 20),
        cost_estimate=pl.CostEstimate(
            flops=4 * norb * rows * WINDOW * parts * width,
            bytes_accessed=4 * norb * rows * WINDOW,
            transcendentals=0,
        ),
    )(own, other, *flat, *old)
    pairs = [(new[2 * j], new[2 * j + 1]) for j in range(parts)]
    return (pairs, new[-1]) if keep else pairs


def finish_kernel(place_ref, mine_ref, theirs_ref, *out_refs):
    norb, _, width = mine_ref.shape
    planes, slots, _ = out_refs[0].shape
    for i in range(norb):
        back = (mine_ref[i] + theirs_ref[i]).astype(jnp.bfloat16)
        out = jnp.dot(place_ref[...], back, preferred_element_type=jnp.float32)
        out = out.astype(jnp.bfloat16).reshape(-1, planes // norb, slots, width)
        for m, out_ref in enumerate(out_refs):
            out_ref[pl.ds(i * (planes // norb), planes // norb)] = out[m]


def finish(place, mine, theirs, shape):
    vmem = pl.BlockSpec(memory_space=pltpu.VMEM)
    count, planes, slots, _ = shape
    part = jax.ShapeDtypeStruct((planes, slots, mine.shape[2]), jnp.bfloat16)
    return pl.pallas_call(
        finish_kernel,
        out_shape=[part] * count,
        in_specs=[vmem] * 3,
        out_specs=[vmem] * count,
        compiler_params=pltpu.CompilerParams(vmem_limit_bytes=20 << 20),
        cost_estimate=pl.CostEstimate(
            flops=2 * count * part.size * place.shape[1],
            bytes_accessed=2 * count * part.size,
            transcendentals=0,
        ),
    )(place, mine, theirs)


def exchange_order(count):
    far = list(range(count // 2, count))
    near = list(range(count // 2))
    return [m for pair in zip(far, near) for m in pair]


def settle_kernel(*refs):
    out_ref = refs[-1]
    count, _, _, naux = out_ref.shape
    width = naux // HALVES
    me = lax.axis_index("wide")
    for j in range(HALVES):
        for k, m in enumerate(exchange_order(count)):
            out_ref[me ^ m, :, :, pl.ds(j * width, width)] = refs[j * count + k][...]


def settle(arrived, shape):
    vmem = pl.BlockSpec(memory_space=pltpu.VMEM)
    flat = [value for part in arrived for value in part]
    return pl.pallas_call(
        settle_kernel,
        out_shape=jax.ShapeDtypeStruct(shape, jnp.bfloat16),
        in_specs=[vmem] * len(flat),
        out_specs=vmem,
        compiler_params=pltpu.CompilerParams(vmem_limit_bytes=20 << 20),
        cost_estimate=pl.CostEstimate(
            flops=0, bytes_accessed=4 * math.prod(shape), transcendentals=0
        ),
    )(*flat)


def ring_products(gamma, coefficients, ids, place, shape):
    count = lax.axis_size("wide")
    norb, depth, naux = gamma.shape
    width = naux // HALVES
    swap = [(d, d ^ 1) for d in range(count)]
    other = lax.ppermute(coefficients, "wide", swap)

    piece = [
        [gamma[i, :, j * width : (j + 1) * width] for i in range(norb)] for j in range(HALVES)
    ]
    shift = [
        [
            (2 * ring_chip(p) + k, 2 * ring_chip(p + way) + k)
            for p in range(GRID_CHIPS)
            for k in range(2)
        ]
        for way in WAYS
    ]
    arrived, sums, done = [], [], 0
    for t in range(GRID_CHIPS):
        arrived.append([list(part) for part in piece])
        if t + 1 == GRID_CHIPS:
            break
        for j in range(HALVES):
            while done < BEHIND[t][j]:
                sums = add_products(done, coefficients, other, arrived[done], sums)
                done += 1
            for i in range(norb):
                sent = piece[j][i]
                if t == 2 and i == j == 0:
                    sent, ids, place = lax.optimization_barrier((sent, ids, place))
                if BEHIND[t][j]:
                    sent, sums = lax.optimization_barrier((sent, sums))
                piece[j][i] = lax.ppermute(sent, "wide", shift[i])
    while done < GRID_CHIPS - 1:
        sums = add_products(done, coefficients, other, arrived[done], sums)
        done += 1
    sums[:1], windows = add_products(
        done, coefficients, other, arrived[done][:1], sums[:1], keep=True
    )
    sums[1] = add_last_products(done, windows, arrived[done][1], sums[1])
    landed = []
    for j in range(HALVES):
        theirs = lax.ppermute(sums[j][1], "wide", swap)
        parts = finish(place, sums[j][0], theirs, shape)
        landed.append(
            [
                lax.ppermute(parts[m], "wide", [(d, d ^ m) for d in range(count)])
                if m
                else parts[m]
                for m in exchange_order(count)
            ]
        )
    return ids, settle(landed, shape)


def local(gamma, coefficients, owners):
    count = lax.axis_size("wide")
    blocks_here = owners.shape[0]
    slots = max(2, 2 * blocks_here // count)
    block_rows = coefficients.shape[0] // blocks_here
    norb, depth, naux = gamma.shape
    shape = (count, norb * block_rows, slots, naux)

    ring = count == 2 * GRID_CHIPS and norb == len(WAYS)
    mask = lax.axis_index("wide") if ring else 0
    labels, place = routing(owners, count, slots, block_rows, mask)
    ids = lax.all_to_all(labels, "wide", split_axis=0, concat_axis=0, tiled=True)
    if ring:
        ids, placed = ring_products(gamma, coefficients, ids, place, shape)
    else:
        gathered = lax.all_gather(gamma, "wide", axis=1, tiled=True)
        back = jnp.einsum(
            "ra,ian->irn", coefficients, gathered, preferred_element_type=jnp.float32
        ).astype(jnp.bfloat16)
        out = jnp.einsum("tr,irn->itn", place, back, preferred_element_type=jnp.float32)
        out = out.astype(jnp.bfloat16).reshape(norb, count, block_rows, slots, naux)
        out = out.transpose(1, 0, 2, 3, 4).reshape(shape)
        placed = lax.all_to_all(out, "wide", split_axis=0, concat_axis=0, tiled=True)
    return placed.transpose(0, 2, 1, 3)[None], ids[None]


def solution(mesh):
    placed = (P("groups", "wide", None), P("wide", None), P("wide", None))
    return jax.shard_map(
        local,
        mesh=mesh,
        in_specs=placed,
        out_specs=(P("wide", None, "groups", None, None), P("wide", "groups", None)),
        check_vma=False,
    )
```

```python
import functools
import math

import jax
import jax.numpy as jnp
from jax import lax
from jax.experimental import pallas as pl
from jax.experimental.pallas import tpu as pltpu
from jax.sharding import PartitionSpec as P

GRID_CHIPS = 8
HALVES = 2
BEHIND = ((0, 0), (0, 0), (0, 1), (1, 2), (2, 4), (4, 5), (5, 6))
WAYS = (1, -1)
LANES = 128
WINDOW = 896


def ring_chip(at):
    at = at % GRID_CHIPS
    back = 2 * ((GRID_CHIPS - at) % GRID_CHIPS)
    up = 2 * at - 1
    if isinstance(at, int):
        return up if 1 <= at <= GRID_CHIPS // 2 else back
    return jnp.where((at >= 1) & (at <= GRID_CHIPS // 2), up, back)


def ring_place(chip):
    z, y = chip // 2, chip % 2
    return jnp.where(y == 1, 1 + z, (GRID_CHIPS - z) % GRID_CHIPS)


def routing(owners, count, slots, block_rows):
    blocks_here = owners.shape[0]
    rows = blocks_here * block_rows
    owner_col = owners[:, 0]
    same = owner_col[:, None] == owner_col[None, :]
    lower = jnp.arange(blocks_here)[:, None] > jnp.arange(blocks_here)[None, :]
    rank = jnp.sum((same & lower).astype(jnp.int32), axis=1)
    target = owner_col * slots + rank
    select = jnp.arange(count * slots, dtype=jnp.int32)[:, None] == target[None, :]
    global_ids = lax.axis_index("wide") * blocks_here + jnp.arange(blocks_here, dtype=jnp.int32)
    labels = jnp.sum(jnp.where(select, global_ids[None, :] + 1, 0), axis=1) - 1
    row_at = jnp.arange(rows, dtype=jnp.int32)
    out_at = jnp.arange(count * block_rows * slots, dtype=jnp.int32)
    row_key = jnp.repeat(target, block_rows) * block_rows + row_at % block_rows
    out_key = (
        out_at // (block_rows * slots) * slots + out_at % slots
    ) * block_rows + out_at // slots % block_rows
    place = (out_key[:, None] == row_key[None, :]).astype(jnp.bfloat16)
    return labels.reshape(count, slots), place


def window_at(start, nvirt):
    return jnp.minimum(start // LANES * LANES, nvirt - WINDOW)


def step_kernel(t, parts, own_hbm, other_hbm, *refs):
    norb = len(WAYS)
    pieces = refs[: norb * parts]
    c_buf, g_buf, sems = refs[-3:]
    sums = refs[-3 - 2 * parts : -3]
    before = refs[norb * parts : -3 - 2 * parts]
    rows, nvirt = own_hbm.shape
    depth, width = pieces[0].shape
    me = lax.axis_index("wide")
    core = lax.rem(me, 2)
    here = ring_place(lax.div(me, 2))
    shifts, copies = [], []
    for i in range(norb):
        chip = ring_chip(here - t * WAYS[i] + GRID_CHIPS)
        start = (2 * chip + core) * depth
        at = pl.multiple_of(window_at(start, nvirt), LANES)
        shifts.append(pl.multiple_of(start - at, 16))
        columns = pl.ds(at, WINDOW)
        copies.append(
            [
                pltpu.make_async_copy(
                    source.at[:, columns], c_buf.at[i, pl.ds(k * rows, rows)], sems.at[i, k]
                )
                for k, source in enumerate((own_hbm, other_hbm))
            ]
        )
        for copy in copies[i]:
            copy.start()
    for i in range(norb):
        g_buf[i] = jnp.zeros_like(g_buf[i])
        for j in range(parts):
            g_buf[i, pl.ds(shifts[i], depth), pl.ds(j * width, width)] = pieces[
                j * norb + i
            ][...]
    for i in range(norb):
        for copy in copies[i]:
            copy.wait()
        for k in range(2):
            term = jnp.dot(
                c_buf[i, pl.ds(k * rows, rows)], g_buf[i], preferred_element_type=jnp.float32
            )
            for j in range(parts):
                part = term[:, j * width : (j + 1) * width]
                at = 2 * j + k
                sums[at][i] = before[at][i] + part if before else part


def last_kernel(t, c_ref, *refs):
    norb = len(WAYS)
    pieces, before, sums, g_buf = refs[:norb], refs[norb : norb + 2], refs[-3:-1], refs[-1]
    rows = before[0].shape[1]
    depth = pieces[0].shape[0]
    nvirt = depth * 2 * GRID_CHIPS
    me = lax.axis_index("wide")
    for i in range(norb):
        chip = ring_chip(ring_place(lax.div(me, 2)) - t * WAYS[i] + GRID_CHIPS)
        start = (2 * chip + lax.rem(me, 2)) * depth
        shift = pl.multiple_of(start - window_at(start, nvirt), 16)
        g_buf[i] = jnp.zeros_like(g_buf[i])
        g_buf[i, pl.ds(shift, depth), :] = pieces[i][...]
    for i in range(norb):
        for k in range(2):
            term = jnp.dot(
                c_ref[i, pl.ds(k * rows, rows)], g_buf[i], preferred_element_type=jnp.float32
            )
            sums[k][i] = before[k][i] + term


def add_last_products(t, windows, pieces, before):
    norb = len(WAYS)
    depth, width = pieces[0].shape
    vmem = pl.BlockSpec(memory_space=pltpu.VMEM)
    sums = jax.ShapeDtypeStruct(before[0].shape, jnp.float32)
    return pl.pallas_call(
        functools.partial(last_kernel, t),
        out_shape=[sums] * 2,
        in_specs=[vmem] * (1 + norb + 2),
        out_specs=[vmem] * 2,
        input_output_aliases={1 + norb + k: k for k in range(2)},
        scratch_shapes=[pltpu.VMEM((norb, WINDOW, width), jnp.bfloat16)],
        compiler_params=pltpu.CompilerParams(vmem_limit_bytes=20 << 20),
        cost_estimate=pl.CostEstimate(
            flops=2 * windows.size * width,
            bytes_accessed=2 * windows.size,
            transcendentals=0,
        ),
    )(windows, *pieces, *before)


def add_products(t, own, other, pieces, before, keep=False):
    rows, nvirt = own.shape
    parts, norb = len(pieces), len(WAYS)
    depth, width = pieces[0][0].shape
    sums = jax.ShapeDtypeStruct((norb, rows, width), jnp.float32)
    vmem = pl.BlockSpec(memory_space=pltpu.VMEM)
    hbm = pl.BlockSpec(memory_space=pltpu.HBM)
    flat = [piece for part in pieces for piece in part]
    old = [value for pair in before for value in pair]
    windows = (norb, 2 * rows, WINDOW)
    kept = [jax.ShapeDtypeStruct(windows, own.dtype)] * keep
    new = pl.pallas_call(
        functools.partial(step_kernel, t, parts),
        out_shape=[sums] * (2 * parts) + kept,
        in_specs=[hbm, hbm] + [vmem] * (len(flat) + len(old)),
        out_specs=[vmem] * (2 * parts + keep),
        input_output_aliases={2 + len(flat) + k: k for k in range(len(old))},
        scratch_shapes=[pltpu.VMEM(windows, own.dtype)] * (not keep)
        + [
            pltpu.VMEM((norb, WINDOW, parts * width), jnp.bfloat16),
            pltpu.SemaphoreType.DMA((norb, 2)),
        ],
        compiler_params=pltpu.CompilerParams(vmem_limit_bytes=20 << 20),
        cost_estimate=pl.CostEstimate(
            flops=4 * norb * rows * WINDOW * parts * width,
            bytes_accessed=4 * norb * rows * WINDOW,
            transcendentals=0,
        ),
    )(own, other, *flat, *old)
    pairs = [(new[2 * j], new[2 * j + 1]) for j in range(parts)]
    return (pairs, new[-1]) if keep else pairs


def finish_kernel(half, place_ref, mine_ref, theirs_ref, *refs):
    out_hbm, buf, sems = refs[-3:]
    norb, _, width = mine_ref.shape
    _, planes, slots, _ = out_hbm.shape
    columns = pl.ds(half * width, width)
    copies = []
    for i in range(norb):
        back = (mine_ref[i] + theirs_ref[i]).astype(jnp.bfloat16)
        out = jnp.dot(place_ref[...], back, preferred_element_type=jnp.float32)
        plane = pl.ds(i * (planes // norb), planes // norb)
        buf[:, plane] = out.astype(jnp.bfloat16).reshape(-1, planes // norb, slots, width)
        copies.append(
            pltpu.make_async_copy(
                buf.at[:, plane], out_hbm.at[:, plane, :, columns], sems.at[i]
            )
        )
        copies[i].start()
    for copy in copies:
        copy.wait()


def finish(half, place, mine, theirs, before, shape):
    vmem = pl.BlockSpec(memory_space=pltpu.VMEM)
    hbm = pl.BlockSpec(memory_space=pltpu.HBM)
    norb, _, width = mine.shape
    return pl.pallas_call(
        functools.partial(finish_kernel, half),
        out_shape=jax.ShapeDtypeStruct(shape, jnp.bfloat16),
        in_specs=[vmem] * 3 + [hbm] * len(before),
        out_specs=hbm,
        input_output_aliases={3: 0} if before else {},
        scratch_shapes=[
            pltpu.VMEM(shape[:3] + (width,), jnp.bfloat16),
            pltpu.SemaphoreType.DMA((norb,)),
        ],
        compiler_params=pltpu.CompilerParams(vmem_limit_bytes=20 << 20),
        cost_estimate=pl.CostEstimate(
            flops=math.prod(shape) * place.shape[1],
            bytes_accessed=2 * math.prod(shape),
            transcendentals=0,
        ),
    )(place, mine, theirs, *before)


def store_kernel(value_ref, out_hbm, sem):
    copy = pltpu.make_async_copy(value_ref, out_hbm, sem)
    copy.start()
    copy.wait()


def store(value):
    return pl.pallas_call(
        store_kernel,
        out_shape=jax.ShapeDtypeStruct(value.shape, value.dtype),
        in_specs=[pl.BlockSpec(memory_space=pltpu.VMEM)],
        out_specs=pl.BlockSpec(memory_space=pltpu.HBM),
        scratch_shapes=[pltpu.SemaphoreType.DMA],
    )(value)


def ring_products(gamma, coefficients, ids, place, shape):
    count = lax.axis_size("wide")
    norb, depth, naux = gamma.shape
    width = naux // HALVES
    swap = [(d, d ^ 1) for d in range(count)]
    other = lax.ppermute(coefficients, "wide", swap)

    piece = [
        [gamma[i, :, j * width : (j + 1) * width] for i in range(norb)] for j in range(HALVES)
    ]
    shift = [
        [
            (2 * ring_chip(p) + k, 2 * ring_chip(p + way) + k)
            for p in range(GRID_CHIPS)
            for k in range(2)
        ]
        for way in WAYS
    ]
    arrived, sums, done = [], [], 0
    for t in range(GRID_CHIPS):
        arrived.append([list(part) for part in piece])
        if t + 1 == GRID_CHIPS:
            break
        for j in range(HALVES):
            while done < BEHIND[t][j]:
                sums = add_products(done, coefficients, other, arrived[done], sums)
                done += 1
            for i in range(norb):
                sent = piece[j][i]
                if t == 2 and i == j == 0:
                    sent, ids, place = lax.optimization_barrier((sent, ids, place))
                if BEHIND[t][j]:
                    sent, sums = lax.optimization_barrier((sent, sums))
                piece[j][i] = lax.ppermute(sent, "wide", shift[i])
    while done < GRID_CHIPS - 1:
        sums = add_products(done, coefficients, other, arrived[done], sums)
        done += 1
    sums[:1], windows = add_products(
        done, coefficients, other, arrived[done][:1], sums[:1], keep=True
    )
    sums[1] = add_last_products(done, windows, arrived[done][1], sums[1])
    theirs = [lax.ppermute(sums[j][1], "wide", swap) for j in range(HALVES)]
    out = []
    for j in range(HALVES):
        out = [finish(j, place, sums[j][0], theirs[j], out, shape)]
    return store(ids), out[0]


def local(gamma, coefficients, owners):
    count = lax.axis_size("wide")
    blocks_here = owners.shape[0]
    slots = max(2, 2 * blocks_here // count)
    block_rows = coefficients.shape[0] // blocks_here
    norb, depth, naux = gamma.shape
    shape = (count, norb * block_rows, slots, naux)

    labels, place = routing(owners, count, slots, block_rows)
    ids = lax.all_to_all(labels, "wide", split_axis=0, concat_axis=0, tiled=True)
    if count == 2 * GRID_CHIPS and norb == len(WAYS):
        ids, out = ring_products(gamma, coefficients, ids, place, shape)
    else:
        gathered = lax.all_gather(gamma, "wide", axis=1, tiled=True)
        back = jnp.einsum(
            "ra,ian->irn", coefficients, gathered, preferred_element_type=jnp.float32
        ).astype(jnp.bfloat16)
        out = jnp.einsum("tr,irn->itn", place, back, preferred_element_type=jnp.float32)
        out = out.astype(jnp.bfloat16).reshape(norb, count, block_rows, slots, naux)
        out = out.transpose(1, 0, 2, 3, 4).reshape(shape)
    placed = lax.all_to_all(out, "wide", split_axis=0, concat_axis=0, tiled=True)
    return placed.transpose(0, 2, 1, 3)[None], ids[None]


def solution(mesh):
    placed = (P("groups", "wide", None), P("wide", None), P("wide", None))
    return jax.shard_map(
        local,
        mesh=mesh,
        in_specs=placed,
        out_specs=(P("wide", None, "groups", None, None), P("wide", "groups", None)),
        check_vma=False,
    )
```

```python
import functools
import math

import jax
import jax.numpy as jnp
from jax import lax
from jax.experimental import pallas as pl
from jax.experimental.pallas import tpu as pltpu
from jax.sharding import PartitionSpec as P

GRID_CHIPS = 8
HALVES = 2
BEHIND = ((0, 0), (0, 0), (0, 1), (1, 2), (2, 4), (4, 5), (5, 6))
WAYS = (1, -1)
LANES = 128
WINDOW = 896


def ring_chip(at):
    at = at % GRID_CHIPS
    back = 2 * ((GRID_CHIPS - at) % GRID_CHIPS)
    up = 2 * at - 1
    if isinstance(at, int):
        return up if 1 <= at <= GRID_CHIPS // 2 else back
    return jnp.where((at >= 1) & (at <= GRID_CHIPS // 2), up, back)


def ring_place(chip):
    z, y = chip // 2, chip % 2
    return jnp.where(y == 1, 1 + z, (GRID_CHIPS - z) % GRID_CHIPS)


def routing(owners, count, slots, block_rows):
    blocks_here = owners.shape[0]
    rows = blocks_here * block_rows
    owner_col = owners[:, 0]
    same = owner_col[:, None] == owner_col[None, :]
    lower = jnp.arange(blocks_here)[:, None] > jnp.arange(blocks_here)[None, :]
    rank = jnp.sum((same & lower).astype(jnp.int32), axis=1)
    target = owner_col * slots + rank
    select = jnp.arange(count * slots, dtype=jnp.int32)[:, None] == target[None, :]
    global_ids = lax.axis_index("wide") * blocks_here + jnp.arange(blocks_here, dtype=jnp.int32)
    labels = jnp.sum(jnp.where(select, global_ids[None, :] + 1, 0), axis=1) - 1
    row_at = jnp.arange(rows, dtype=jnp.int32)
    out_at = jnp.arange(count * block_rows * slots, dtype=jnp.int32)
    row_key = jnp.repeat(target, block_rows) * block_rows + row_at % block_rows
    out_key = (
        out_at // (block_rows * slots) * slots + out_at % slots
    ) * block_rows + out_at // slots % block_rows
    place = (out_key[:, None] == row_key[None, :]).astype(jnp.bfloat16)
    return labels.reshape(count, slots), place


def window_at(start, nvirt):
    return jnp.minimum(start // LANES * LANES, nvirt - WINDOW)


def step_kernel(t, parts, own_hbm, other_hbm, *refs):
    norb = len(WAYS)
    pieces = refs[: norb * parts]
    c_buf, g_buf, sems = refs[-3:]
    sums = refs[-3 - 2 * parts : -3]
    before = refs[norb * parts : -3 - 2 * parts]
    rows, nvirt = own_hbm.shape
    depth, width = pieces[0].shape
    me = lax.axis_index("wide")
    core = lax.rem(me, 2)
    here = ring_place(lax.div(me, 2))
    shifts, copies = [], []
    for i in range(norb):
        chip = ring_chip(here - t * WAYS[i] + GRID_CHIPS)
        start = (2 * chip + core) * depth
        at = pl.multiple_of(window_at(start, nvirt), LANES)
        shifts.append(pl.multiple_of(start - at, 16))
        columns = pl.ds(at, WINDOW)
        copies.append(
            [
                pltpu.make_async_copy(
                    source.at[:, columns], c_buf.at[i, pl.ds(k * rows, rows)], sems.at[i, k]
                )
                for k, source in enumerate((own_hbm, other_hbm))
            ]
        )
        for copy in copies[i]:
            copy.start()
    for i in range(norb):
        g_buf[i] = jnp.zeros_like(g_buf[i])
        for j in range(parts):
            g_buf[i, pl.ds(shifts[i], depth), pl.ds(j * width, width)] = pieces[
                j * norb + i
            ][...]
    for i in range(norb):
        for copy in copies[i]:
            copy.wait()
        for k in range(2):
            term = jnp.dot(
                c_buf[i, pl.ds(k * rows, rows)], g_buf[i], preferred_element_type=jnp.float32
            )
            for j in range(parts):
                part = term[:, j * width : (j + 1) * width]
                at = 2 * j + k
                sums[at][i] = before[at][i] + part if before else part


def last_kernel(t, c_ref, *refs):
    norb = len(WAYS)
    pieces, before, sums, g_buf = refs[:norb], refs[norb : norb + 2], refs[-3:-1], refs[-1]
    rows = before[0].shape[1]
    depth = pieces[0].shape[0]
    nvirt = depth * 2 * GRID_CHIPS
    me = lax.axis_index("wide")
    for i in range(norb):
        chip = ring_chip(ring_place(lax.div(me, 2)) - t * WAYS[i] + GRID_CHIPS)
        start = (2 * chip + lax.rem(me, 2)) * depth
        shift = pl.multiple_of(start - window_at(start, nvirt), 16)
        g_buf[i] = jnp.zeros_like(g_buf[i])
        g_buf[i, pl.ds(shift, depth), :] = pieces[i][...]
    for i in range(norb):
        for k in range(2):
            term = jnp.dot(
                c_ref[i, pl.ds(k * rows, rows)], g_buf[i], preferred_element_type=jnp.float32
            )
            sums[k][i] = before[k][i] + term


def add_last_products(t, windows, pieces, before):
    norb = len(WAYS)
    depth, width = pieces[0].shape
    vmem = pl.BlockSpec(memory_space=pltpu.VMEM)
    sums = jax.ShapeDtypeStruct(before[0].shape, jnp.float32)
    return pl.pallas_call(
        functools.partial(last_kernel, t),
        out_shape=[sums] * 2,
        in_specs=[vmem] * (1 + norb + 2),
        out_specs=[vmem] * 2,
        input_output_aliases={1 + norb + k: k for k in range(2)},
        scratch_shapes=[pltpu.VMEM((norb, WINDOW, width), jnp.bfloat16)],
        compiler_params=pltpu.CompilerParams(vmem_limit_bytes=20 << 20),
        cost_estimate=pl.CostEstimate(
            flops=2 * windows.size * width,
            bytes_accessed=2 * windows.size,
            transcendentals=0,
        ),
    )(windows, *pieces, *before)


def add_products(t, own, other, pieces, before, keep=False):
    rows, nvirt = own.shape
    parts, norb = len(pieces), len(WAYS)
    depth, width = pieces[0][0].shape
    sums = jax.ShapeDtypeStruct((norb, rows, width), jnp.float32)
    vmem = pl.BlockSpec(memory_space=pltpu.VMEM)
    hbm = pl.BlockSpec(memory_space=pltpu.HBM)
    flat = [piece for part in pieces for piece in part]
    old = [value for pair in before for value in pair]
    windows = (norb, 2 * rows, WINDOW)
    kept = [jax.ShapeDtypeStruct(windows, own.dtype)] * keep
    new = pl.pallas_call(
        functools.partial(step_kernel, t, parts),
        out_shape=[sums] * (2 * parts) + kept,
        in_specs=[hbm, hbm] + [vmem] * (len(flat) + len(old)),
        out_specs=[vmem] * (2 * parts + keep),
        input_output_aliases={2 + len(flat) + k: k for k in range(len(old))},
        scratch_shapes=[pltpu.VMEM(windows, own.dtype)] * (not keep)
        + [
            pltpu.VMEM((norb, WINDOW, parts * width), jnp.bfloat16),
            pltpu.SemaphoreType.DMA((norb, 2)),
        ],
        compiler_params=pltpu.CompilerParams(vmem_limit_bytes=20 << 20),
        cost_estimate=pl.CostEstimate(
            flops=4 * norb * rows * WINDOW * parts * width,
            bytes_accessed=4 * norb * rows * WINDOW,
            transcendentals=0,
        ),
    )(own, other, *flat, *old)
    pairs = [(new[2 * j], new[2 * j + 1]) for j in range(parts)]
    return (pairs, new[-1]) if keep else pairs


def finish_kernel(half, place_ref, mine_ref, theirs_ref, *refs):
    out_hbm, buf, sems = refs[-3:]
    norb, _, width = mine_ref.shape
    _, planes, slots, _ = out_hbm.shape
    columns = pl.ds(half * width, width)
    copies = []
    for i in range(norb):
        back = (mine_ref[i] + theirs_ref[i]).astype(jnp.bfloat16)
        out = jnp.dot(place_ref[...], back, preferred_element_type=jnp.float32)
        plane = pl.ds(i * (planes // norb), planes // norb)
        buf[:, plane] = out.astype(jnp.bfloat16).reshape(-1, planes // norb, slots, width)
        copies.append(
            pltpu.make_async_copy(
                buf.at[:, plane], out_hbm.at[:, plane, :, columns], sems.at[i]
            )
        )
        copies[i].start()
    for copy in copies:
        copy.wait()


def finish(half, place, mine, theirs, before, shape):
    vmem = pl.BlockSpec(memory_space=pltpu.VMEM)
    hbm = pl.BlockSpec(memory_space=pltpu.HBM)
    norb, _, width = mine.shape
    return pl.pallas_call(
        functools.partial(finish_kernel, half),
        out_shape=jax.ShapeDtypeStruct(shape, jnp.bfloat16),
        in_specs=[vmem] * 3 + [hbm] * len(before),
        out_specs=hbm,
        input_output_aliases={3: 0} if before else {},
        scratch_shapes=[
            pltpu.VMEM(shape[:3] + (width,), jnp.bfloat16),
            pltpu.SemaphoreType.DMA((norb,)),
        ],
        compiler_params=pltpu.CompilerParams(vmem_limit_bytes=20 << 20),
        cost_estimate=pl.CostEstimate(
            flops=math.prod(shape) * place.shape[1],
            bytes_accessed=2 * math.prod(shape),
            transcendentals=0,
        ),
    )(place, mine, theirs, *before)


def store_kernel(value_ref, out_hbm, sem):
    copy = pltpu.make_async_copy(value_ref, out_hbm, sem)
    copy.start()
    copy.wait()


def store(value):
    return pl.pallas_call(
        store_kernel,
        out_shape=jax.ShapeDtypeStruct(value.shape, value.dtype),
        in_specs=[pl.BlockSpec(memory_space=pltpu.VMEM)],
        out_specs=pl.BlockSpec(memory_space=pltpu.HBM),
        scratch_shapes=[pltpu.SemaphoreType.DMA],
    )(value)


def exchange(value):
    return lax.all_to_all(value, "wide", split_axis=0, concat_axis=0, tiled=True)


def ring_products(gamma, coefficients, labels, place, shape):
    count = lax.axis_size("wide")
    norb, depth, naux = gamma.shape
    width = naux // HALVES
    swap = [(d, d ^ 1) for d in range(count)]
    other = lax.ppermute(coefficients, "wide", swap)

    piece = []
    for j in range(HALVES):
        if j:
            gamma, place = lax.optimization_barrier((gamma, place))
        piece.append([gamma[i, :, j * width : (j + 1) * width] for i in range(norb)])
    shift = [
        [
            (2 * ring_chip(p) + k, 2 * ring_chip(p + way) + k)
            for p in range(GRID_CHIPS)
            for k in range(2)
        ]
        for way in WAYS
    ]
    arrived, sums, done = [], [], 0
    for t in range(GRID_CHIPS):
        arrived.append([list(part) for part in piece])
        if t + 1 == GRID_CHIPS:
            break
        for j in range(HALVES):
            while done < BEHIND[t][j]:
                sums = add_products(done, coefficients, other, arrived[done], sums)
                done += 1
            for i in range(norb):
                sent = piece[j][i]
                if t == 1 and i == j == HALVES - 1:
                    sent, labels = lax.optimization_barrier((sent, labels))
                    ids = exchange(labels)
                if t == 3 and i == j == 0:
                    sent, ids = lax.optimization_barrier((sent, ids))
                if BEHIND[t][j]:
                    sent, sums = lax.optimization_barrier((sent, sums))
                piece[j][i] = lax.ppermute(sent, "wide", shift[i])
    while done < GRID_CHIPS - 1:
        sums = add_products(done, coefficients, other, arrived[done], sums)
        done += 1
    sums[:1], windows = add_products(
        done, coefficients, other, arrived[done][:1], sums[:1], keep=True
    )
    sums[1] = add_last_products(done, windows, arrived[done][1], sums[1])
    theirs = [lax.ppermute(sums[j][1], "wide", swap) for j in range(HALVES)]
    out = []
    for j in range(HALVES):
        out = [finish(j, place, sums[j][0], theirs[j], out, shape)]
    return store(ids), out[0]


def local(gamma, coefficients, owners):
    count = lax.axis_size("wide")
    blocks_here = owners.shape[0]
    slots = max(2, 2 * blocks_here // count)
    block_rows = coefficients.shape[0] // blocks_here
    norb, depth, naux = gamma.shape
    shape = (count, norb * block_rows, slots, naux)

    labels, place = routing(owners, count, slots, block_rows)
    if count == 2 * GRID_CHIPS and norb == len(WAYS):
        ids, out = ring_products(gamma, coefficients, labels, place, shape)
    else:
        gathered = lax.all_gather(gamma, "wide", axis=1, tiled=True)
        back = jnp.einsum(
            "ra,ian->irn", coefficients, gathered, preferred_element_type=jnp.float32
        ).astype(jnp.bfloat16)
        out = jnp.einsum("tr,irn->itn", place, back, preferred_element_type=jnp.float32)
        out = out.astype(jnp.bfloat16).reshape(norb, count, block_rows, slots, naux)
        out = out.transpose(1, 0, 2, 3, 4).reshape(shape)
        ids = exchange(labels)
    placed = exchange(out)
    return placed.transpose(0, 2, 1, 3)[None], ids[None]


def solution(mesh):
    placed = (P("groups", "wide", None), P("wide", None), P("wide", None))
    return jax.shard_map(
        local,
        mesh=mesh,
        in_specs=placed,
        out_specs=(P("wide", None, "groups", None, None), P("wide", "groups", None)),
        check_vma=False,
    )
```

```python
import functools
import math

import jax
import jax.numpy as jnp
from jax import lax
from jax.experimental import pallas as pl
from jax.experimental.pallas import tpu as pltpu
from jax.sharding import PartitionSpec as P

GRID_CHIPS = 8
HALVES = 2
BEHIND = ((0, 0), (0, 0), (0, 1), (1, 2), (2, 4), (4, 5), (5, 6))
WAYS = (1, -1)
LANES = 128
WINDOW = 896


def ring_chip(at):
    at = at % GRID_CHIPS
    back = 2 * ((GRID_CHIPS - at) % GRID_CHIPS)
    up = 2 * at - 1
    if isinstance(at, int):
        return up if 1 <= at <= GRID_CHIPS // 2 else back
    return jnp.where((at >= 1) & (at <= GRID_CHIPS // 2), up, back)


def ring_place(chip):
    z, y = chip // 2, chip % 2
    return jnp.where(y == 1, 1 + z, (GRID_CHIPS - z) % GRID_CHIPS)


def routing(owners, count, slots, block_rows):
    blocks_here = owners.shape[0]
    rows = blocks_here * block_rows
    owner_col = owners[:, 0]
    same = owner_col[:, None] == owner_col[None, :]
    lower = jnp.arange(blocks_here)[:, None] > jnp.arange(blocks_here)[None, :]
    rank = jnp.sum((same & lower).astype(jnp.int32), axis=1)
    target = owner_col * slots + rank
    select = jnp.arange(count * slots, dtype=jnp.int32)[:, None] == target[None, :]
    global_ids = lax.axis_index("wide") * blocks_here + jnp.arange(blocks_here, dtype=jnp.int32)
    labels = jnp.sum(jnp.where(select, global_ids[None, :] + 1, 0), axis=1) - 1
    row_at = jnp.arange(rows, dtype=jnp.int32)
    out_at = jnp.arange(count * block_rows * slots, dtype=jnp.int32)
    row_key = jnp.repeat(target, block_rows) * block_rows + row_at % block_rows
    out_key = (
        out_at // (block_rows * slots) * slots + out_at % slots
    ) * block_rows + out_at // slots % block_rows
    place = (out_key[:, None] == row_key[None, :]).astype(jnp.bfloat16)
    return labels.reshape(count, slots), place


def window_at(start, nvirt):
    return jnp.minimum(start // LANES * LANES, nvirt - WINDOW)


def step_kernel(t, parts, own_hbm, other_hbm, *refs):
    norb = len(WAYS)
    pieces = refs[: norb * parts]
    c_buf, g_buf, sems = refs[-3:]
    sums = refs[-3 - 2 * parts : -3]
    before = refs[norb * parts : -3 - 2 * parts]
    rows, nvirt = own_hbm.shape
    depth, width = pieces[0].shape
    me = lax.axis_index("wide")
    core = lax.rem(me, 2)
    here = ring_place(lax.div(me, 2))
    shifts, copies = [], []
    for i in range(norb):
        chip = ring_chip(here - t * WAYS[i] + GRID_CHIPS)
        start = (2 * chip + core) * depth
        at = pl.multiple_of(window_at(start, nvirt), LANES)
        shifts.append(pl.multiple_of(start - at, 16))
        columns = pl.ds(at, WINDOW)
        copies.append(
            [
                pltpu.make_async_copy(
                    source.at[:, columns], c_buf.at[i, pl.ds(k * rows, rows)], sems.at[i, k]
                )
                for k, source in enumerate((own_hbm, other_hbm))
            ]
        )
        for copy in copies[i]:
            copy.start()
    for i in range(norb):
        g_buf[i] = jnp.zeros_like(g_buf[i])
        for j in range(parts):
            g_buf[i, pl.ds(shifts[i], depth), pl.ds(j * width, width)] = pieces[
                j * norb + i
            ][...]
    for i in range(norb):
        for copy in copies[i]:
            copy.wait()
        for k in range(2):
            term = jnp.dot(
                c_buf[i, pl.ds(k * rows, rows)], g_buf[i], preferred_element_type=jnp.float32
            )
            for j in range(parts):
                part = term[:, j * width : (j + 1) * width]
                at = 2 * j + k
                sums[at][i] = before[at][i] + part if before else part


def last_kernel(t, c_ref, *refs):
    norb = len(WAYS)
    pieces, before, sums, g_buf = refs[:norb], refs[norb : norb + 2], refs[-3:-1], refs[-1]
    rows = before[0].shape[1]
    depth = pieces[0].shape[0]
    nvirt = depth * 2 * GRID_CHIPS
    me = lax.axis_index("wide")
    for i in range(norb):
        chip = ring_chip(ring_place(lax.div(me, 2)) - t * WAYS[i] + GRID_CHIPS)
        start = (2 * chip + lax.rem(me, 2)) * depth
        shift = pl.multiple_of(start - window_at(start, nvirt), 16)
        g_buf[i] = jnp.zeros_like(g_buf[i])
        g_buf[i, pl.ds(shift, depth), :] = pieces[i][...]
    for i in range(norb):
        for k in range(2):
            term = jnp.dot(
                c_ref[i, pl.ds(k * rows, rows)], g_buf[i], preferred_element_type=jnp.float32
            )
            sums[k][i] = before[k][i] + term


def add_last_products(t, windows, pieces, before):
    norb = len(WAYS)
    depth, width = pieces[0].shape
    vmem = pl.BlockSpec(memory_space=pltpu.VMEM)
    sums = jax.ShapeDtypeStruct(before[0].shape, jnp.float32)
    return pl.pallas_call(
        functools.partial(last_kernel, t),
        out_shape=[sums] * 2,
        in_specs=[vmem] * (1 + norb + 2),
        out_specs=[vmem] * 2,
        input_output_aliases={1 + norb + k: k for k in range(2)},
        scratch_shapes=[pltpu.VMEM((norb, WINDOW, width), jnp.bfloat16)],
        compiler_params=pltpu.CompilerParams(vmem_limit_bytes=20 << 20),
        cost_estimate=pl.CostEstimate(
            flops=2 * windows.size * width,
            bytes_accessed=2 * windows.size,
            transcendentals=0,
        ),
    )(windows, *pieces, *before)


def add_products(t, own, other, pieces, before, keep=False):
    rows, nvirt = own.shape
    parts, norb = len(pieces), len(WAYS)
    depth, width = pieces[0][0].shape
    sums = jax.ShapeDtypeStruct((norb, rows, width), jnp.float32)
    vmem = pl.BlockSpec(memory_space=pltpu.VMEM)
    hbm = pl.BlockSpec(memory_space=pltpu.HBM)
    flat = [piece for part in pieces for piece in part]
    old = [value for pair in before for value in pair]
    windows = (norb, 2 * rows, WINDOW)
    kept = [jax.ShapeDtypeStruct(windows, own.dtype)] * keep
    new = pl.pallas_call(
        functools.partial(step_kernel, t, parts),
        out_shape=[sums] * (2 * parts) + kept,
        in_specs=[hbm, hbm] + [vmem] * (len(flat) + len(old)),
        out_specs=[vmem] * (2 * parts + keep),
        input_output_aliases={2 + len(flat) + k: k for k in range(len(old))},
        scratch_shapes=[pltpu.VMEM(windows, own.dtype)] * (not keep)
        + [
            pltpu.VMEM((norb, WINDOW, parts * width), jnp.bfloat16),
            pltpu.SemaphoreType.DMA((norb, 2)),
        ],
        compiler_params=pltpu.CompilerParams(vmem_limit_bytes=20 << 20),
        cost_estimate=pl.CostEstimate(
            flops=4 * norb * rows * WINDOW * parts * width,
            bytes_accessed=4 * norb * rows * WINDOW,
            transcendentals=0,
        ),
    )(own, other, *flat, *old)
    pairs = [(new[2 * j], new[2 * j + 1]) for j in range(parts)]
    return (pairs, new[-1]) if keep else pairs


def finish_kernel(half, place_ref, mine_ref, theirs_ref, *refs):
    out_hbm, buf, sems = refs[-3:]
    norb, _, width = mine_ref.shape
    _, planes, slots, _ = out_hbm.shape
    columns = pl.ds(half * width, width)
    copies = []
    for i in range(norb):
        back = (mine_ref[i] + theirs_ref[i]).astype(jnp.bfloat16)
        out = jnp.dot(place_ref[...], back, preferred_element_type=jnp.float32)
        plane = pl.ds(i * (planes // norb), planes // norb)
        buf[:, plane] = out.astype(jnp.bfloat16).reshape(-1, planes // norb, slots, width)
        copies.append(
            pltpu.make_async_copy(
                buf.at[:, plane], out_hbm.at[:, plane, :, columns], sems.at[i]
            )
        )
        copies[i].start()
    for copy in copies:
        copy.wait()


def finish(half, place, mine, theirs, before, shape):
    vmem = pl.BlockSpec(memory_space=pltpu.VMEM)
    hbm = pl.BlockSpec(memory_space=pltpu.HBM)
    norb, _, width = mine.shape
    return pl.pallas_call(
        functools.partial(finish_kernel, half),
        out_shape=jax.ShapeDtypeStruct(shape, jnp.bfloat16),
        in_specs=[vmem] * 3 + [hbm] * len(before),
        out_specs=hbm,
        input_output_aliases={3: 0} if before else {},
        scratch_shapes=[
            pltpu.VMEM(shape[:3] + (width,), jnp.bfloat16),
            pltpu.SemaphoreType.DMA((norb,)),
        ],
        compiler_params=pltpu.CompilerParams(vmem_limit_bytes=20 << 20),
        cost_estimate=pl.CostEstimate(
            flops=math.prod(shape) * place.shape[1],
            bytes_accessed=2 * math.prod(shape),
            transcendentals=0,
        ),
    )(place, mine, theirs, *before)


def store_kernel(value_ref, out_hbm, sem):
    copy = pltpu.make_async_copy(value_ref, out_hbm, sem)
    copy.start()
    copy.wait()


def store(value):
    return pl.pallas_call(
        store_kernel,
        out_shape=jax.ShapeDtypeStruct(value.shape, value.dtype),
        in_specs=[pl.BlockSpec(memory_space=pltpu.VMEM)],
        out_specs=pl.BlockSpec(memory_space=pltpu.HBM),
        scratch_shapes=[pltpu.SemaphoreType.DMA],
    )(value)


def exchange(value):
    return lax.all_to_all(value, "wide", split_axis=0, concat_axis=0, tiled=True)


def ring_products(gamma, coefficients, labels, place, shape):
    count = lax.axis_size("wide")
    norb, depth, naux = gamma.shape
    width = naux // HALVES
    swap = [(d, d ^ 1) for d in range(count)]
    other = lax.ppermute(coefficients, "wide", swap)

    ids = exchange(labels)
    piece = []
    for j in range(HALVES):
        if j:
            gamma, place = lax.optimization_barrier((gamma, place))
        piece.append([gamma[i, :, j * width : (j + 1) * width] for i in range(norb)])
    shift = [
        [
            (2 * ring_chip(p) + k, 2 * ring_chip(p + way) + k)
            for p in range(GRID_CHIPS)
            for k in range(2)
        ]
        for way in WAYS
    ]
    arrived, sums, done = [], [], 0
    for t in range(GRID_CHIPS):
        arrived.append([list(part) for part in piece])
        if t + 1 == GRID_CHIPS:
            break
        for j in range(HALVES):
            while done < BEHIND[t][j]:
                sums = add_products(done, coefficients, other, arrived[done], sums)
                done += 1
            for i in range(norb):
                sent = piece[j][i]
                if t == 2 and i == j == 0:
                    sent, ids = lax.optimization_barrier((sent, ids))
                if BEHIND[t][j]:
                    sent, sums = lax.optimization_barrier((sent, sums))
                piece[j][i] = lax.ppermute(sent, "wide", shift[i])
    while done < GRID_CHIPS - 1:
        sums = add_products(done, coefficients, other, arrived[done], sums)
        done += 1
    sums[:1], windows = add_products(
        done, coefficients, other, arrived[done][:1], sums[:1], keep=True
    )
    sums[1] = add_last_products(done, windows, arrived[done][1], sums[1])
    theirs = [lax.ppermute(sums[j][1], "wide", swap) for j in range(HALVES)]
    out = []
    for j in range(HALVES):
        out = [finish(j, place, sums[j][0], theirs[j], out, shape)]
    return store(ids), out[0]


def local(gamma, coefficients, owners):
    count = lax.axis_size("wide")
    blocks_here = owners.shape[0]
    slots = max(2, 2 * blocks_here // count)
    block_rows = coefficients.shape[0] // blocks_here
    norb, depth, naux = gamma.shape
    shape = (count, norb * block_rows, slots, naux)

    labels, place = routing(owners, count, slots, block_rows)
    if count == 2 * GRID_CHIPS and norb == len(WAYS):
        ids, out = ring_products(gamma, coefficients, labels, place, shape)
    else:
        gathered = lax.all_gather(gamma, "wide", axis=1, tiled=True)
        back = jnp.einsum(
            "ra,ian->irn", coefficients, gathered, preferred_element_type=jnp.float32
        ).astype(jnp.bfloat16)
        out = jnp.einsum("tr,irn->itn", place, back, preferred_element_type=jnp.float32)
        out = out.astype(jnp.bfloat16).reshape(norb, count, block_rows, slots, naux)
        out = out.transpose(1, 0, 2, 3, 4).reshape(shape)
        ids = exchange(labels)
    placed = exchange(out)
    return placed.transpose(0, 2, 1, 3)[None], ids[None]


def solution(mesh):
    placed = (P("groups", "wide", None), P("wide", None), P("wide", None))
    return jax.shard_map(
        local,
        mesh=mesh,
        in_specs=placed,
        out_specs=(P("wide", None, "groups", None, None), P("wide", "groups", None)),
        check_vma=False,
    )
```

```python
import functools
import math

import jax
import jax.numpy as jnp
from jax import lax
from jax.experimental import pallas as pl
from jax.experimental.pallas import tpu as pltpu
from jax.sharding import PartitionSpec as P

GRID_CHIPS = 8
HALVES = 2
BEHIND = ((0, 0), (0, 0), (0, 1), (1, 2), (2, 4), (4, 5), (5, 6))
WAYS = (1, -1)
LANES = 128
WINDOW = 896


def ring_chip(at):
    at = at % GRID_CHIPS
    back = 2 * ((GRID_CHIPS - at) % GRID_CHIPS)
    up = 2 * at - 1
    if isinstance(at, int):
        return up if 1 <= at <= GRID_CHIPS // 2 else back
    return jnp.where((at >= 1) & (at <= GRID_CHIPS // 2), up, back)


def ring_place(chip):
    z, y = chip // 2, chip % 2
    return jnp.where(y == 1, 1 + z, (GRID_CHIPS - z) % GRID_CHIPS)


def routing(owners, count, slots, block_rows):
    blocks_here = owners.shape[0]
    rows = blocks_here * block_rows
    owner_col = owners[:, 0]
    same = owner_col[:, None] == owner_col[None, :]
    lower = jnp.arange(blocks_here)[:, None] > jnp.arange(blocks_here)[None, :]
    rank = jnp.sum((same & lower).astype(jnp.int32), axis=1)
    target = owner_col * slots + rank
    select = jnp.arange(count * slots, dtype=jnp.int32)[:, None] == target[None, :]
    global_ids = lax.axis_index("wide") * blocks_here + jnp.arange(blocks_here, dtype=jnp.int32)
    labels = jnp.sum(jnp.where(select, global_ids[None, :] + 1, 0), axis=1) - 1
    row_at = jnp.arange(rows, dtype=jnp.int32)
    out_at = jnp.arange(count * block_rows * slots, dtype=jnp.int32)
    row_key = jnp.repeat(target, block_rows) * block_rows + row_at % block_rows
    out_key = (
        out_at // (block_rows * slots) * slots + out_at % slots
    ) * block_rows + out_at // slots % block_rows
    place = (out_key[:, None] == row_key[None, :]).astype(jnp.bfloat16)
    return labels.reshape(count, slots), place


def window_at(start, nvirt):
    return jnp.minimum(start // LANES * LANES, nvirt - WINDOW)


def step_kernel(t, parts, own_hbm, other_hbm, *refs):
    norb = len(WAYS)
    pieces = refs[: norb * parts]
    c_buf, g_buf, sems = refs[-3:]
    sums = refs[-3 - 2 * parts : -3]
    before = refs[norb * parts : -3 - 2 * parts]
    rows, nvirt = own_hbm.shape
    depth, width = pieces[0].shape
    me = lax.axis_index("wide")
    core = lax.rem(me, 2)
    here = ring_place(lax.div(me, 2))
    shifts, copies = [], []
    for i in range(norb):
        chip = ring_chip(here - t * WAYS[i] + GRID_CHIPS)
        start = (2 * chip + core) * depth
        at = pl.multiple_of(window_at(start, nvirt), LANES)
        shifts.append(pl.multiple_of(start - at, 16))
        columns = pl.ds(at, WINDOW)
        copies.append(
            [
                pltpu.make_async_copy(
                    source.at[:, columns], c_buf.at[i, pl.ds(k * rows, rows)], sems.at[i, k]
                )
                for k, source in enumerate((own_hbm, other_hbm))
            ]
        )
        for copy in copies[i]:
            copy.start()
    for i in range(norb):
        g_buf[i] = jnp.zeros_like(g_buf[i])
        for j in range(parts):
            g_buf[i, pl.ds(shifts[i], depth), pl.ds(j * width, width)] = pieces[
                j * norb + i
            ][...]
    for i in range(norb):
        for copy in copies[i]:
            copy.wait()
        for k in range(2):
            term = jnp.dot(
                c_buf[i, pl.ds(k * rows, rows)], g_buf[i], preferred_element_type=jnp.float32
            )
            for j in range(parts):
                part = term[:, j * width : (j + 1) * width]
                at = 2 * j + k
                sums[at][i] = before[at][i] + part if before else part


def last_kernel(t, c_ref, *refs):
    norb = len(WAYS)
    pieces, before, sums, g_buf = refs[:norb], refs[norb : norb + 2], refs[-3:-1], refs[-1]
    rows = before[0].shape[1]
    depth = pieces[0].shape[0]
    nvirt = depth * 2 * GRID_CHIPS
    me = lax.axis_index("wide")
    for i in range(norb):
        chip = ring_chip(ring_place(lax.div(me, 2)) - t * WAYS[i] + GRID_CHIPS)
        start = (2 * chip + lax.rem(me, 2)) * depth
        shift = pl.multiple_of(start - window_at(start, nvirt), 16)
        g_buf[i] = jnp.zeros_like(g_buf[i])
        g_buf[i, pl.ds(shift, depth), :] = pieces[i][...]
    for i in range(norb):
        for k in range(2):
            term = jnp.dot(
                c_ref[i, pl.ds(k * rows, rows)], g_buf[i], preferred_element_type=jnp.float32
            )
            sums[k][i] = before[k][i] + term


def add_last_products(t, windows, pieces, before):
    norb = len(WAYS)
    depth, width = pieces[0].shape
    vmem = pl.BlockSpec(memory_space=pltpu.VMEM)
    sums = jax.ShapeDtypeStruct(before[0].shape, jnp.float32)
    return pl.pallas_call(
        functools.partial(last_kernel, t),
        out_shape=[sums] * 2,
        in_specs=[vmem] * (1 + norb + 2),
        out_specs=[vmem] * 2,
        input_output_aliases={1 + norb + k: k for k in range(2)},
        scratch_shapes=[pltpu.VMEM((norb, WINDOW, width), jnp.bfloat16)],
        compiler_params=pltpu.CompilerParams(vmem_limit_bytes=20 << 20),
        cost_estimate=pl.CostEstimate(
            flops=2 * windows.size * width,
            bytes_accessed=2 * windows.size,
            transcendentals=0,
        ),
    )(windows, *pieces, *before)


def add_products(t, own, other, pieces, before, keep=False):
    rows, nvirt = own.shape
    parts, norb = len(pieces), len(WAYS)
    depth, width = pieces[0][0].shape
    sums = jax.ShapeDtypeStruct((norb, rows, width), jnp.float32)
    vmem = pl.BlockSpec(memory_space=pltpu.VMEM)
    hbm = pl.BlockSpec(memory_space=pltpu.HBM)
    flat = [piece for part in pieces for piece in part]
    old = [value for pair in before for value in pair]
    windows = (norb, 2 * rows, WINDOW)
    kept = [jax.ShapeDtypeStruct(windows, own.dtype)] * keep
    new = pl.pallas_call(
        functools.partial(step_kernel, t, parts),
        out_shape=[sums] * (2 * parts) + kept,
        in_specs=[hbm, hbm] + [vmem] * (len(flat) + len(old)),
        out_specs=[vmem] * (2 * parts + keep),
        input_output_aliases={2 + len(flat) + k: k for k in range(len(old))},
        scratch_shapes=[pltpu.VMEM(windows, own.dtype)] * (not keep)
        + [
            pltpu.VMEM((norb, WINDOW, parts * width), jnp.bfloat16),
            pltpu.SemaphoreType.DMA((norb, 2)),
        ],
        compiler_params=pltpu.CompilerParams(vmem_limit_bytes=20 << 20),
        cost_estimate=pl.CostEstimate(
            flops=4 * norb * rows * WINDOW * parts * width,
            bytes_accessed=4 * norb * rows * WINDOW,
            transcendentals=0,
        ),
    )(own, other, *flat, *old)
    pairs = [(new[2 * j], new[2 * j + 1]) for j in range(parts)]
    return (pairs, new[-1]) if keep else pairs


def finish_kernel(half, place_ref, mine_ref, theirs_ref, *refs):
    out_hbm, buf, sems = refs[-3:]
    norb, _, width = mine_ref.shape
    _, planes, slots, _ = out_hbm.shape
    columns = pl.ds(half * width, width)
    copies = []
    for i in range(norb):
        back = (mine_ref[i] + theirs_ref[i]).astype(jnp.bfloat16)
        out = jnp.dot(place_ref[...], back, preferred_element_type=jnp.float32)
        plane = pl.ds(i * (planes // norb), planes // norb)
        buf[:, plane] = out.astype(jnp.bfloat16).reshape(-1, planes // norb, slots, width)
        copies.append(
            pltpu.make_async_copy(
                buf.at[:, plane], out_hbm.at[:, plane, :, columns], sems.at[i]
            )
        )
        copies[i].start()
    for copy in copies:
        copy.wait()


def finish(half, place, mine, theirs, before, shape):
    vmem = pl.BlockSpec(memory_space=pltpu.VMEM)
    hbm = pl.BlockSpec(memory_space=pltpu.HBM)
    norb, _, width = mine.shape
    return pl.pallas_call(
        functools.partial(finish_kernel, half),
        out_shape=jax.ShapeDtypeStruct(shape, jnp.bfloat16),
        in_specs=[vmem] * 3 + [hbm] * len(before),
        out_specs=hbm,
        input_output_aliases={3: 0} if before else {},
        scratch_shapes=[
            pltpu.VMEM(shape[:3] + (width,), jnp.bfloat16),
            pltpu.SemaphoreType.DMA((norb,)),
        ],
        compiler_params=pltpu.CompilerParams(vmem_limit_bytes=20 << 20),
        cost_estimate=pl.CostEstimate(
            flops=math.prod(shape) * place.shape[1],
            bytes_accessed=2 * math.prod(shape),
            transcendentals=0,
        ),
    )(place, mine, theirs, *before)


def store_kernel(value_ref, out_hbm, sem):
    copy = pltpu.make_async_copy(value_ref, out_hbm, sem)
    copy.start()
    copy.wait()


def store(value):
    return pl.pallas_call(
        store_kernel,
        out_shape=jax.ShapeDtypeStruct(value.shape, value.dtype),
        in_specs=[pl.BlockSpec(memory_space=pltpu.VMEM)],
        out_specs=pl.BlockSpec(memory_space=pltpu.HBM),
        scratch_shapes=[pltpu.SemaphoreType.DMA],
    )(value)


def exchange(value):
    return lax.all_to_all(value, "wide", split_axis=0, concat_axis=0, tiled=True)


def ring_products(gamma, coefficients, labels, place, shape):
    count = lax.axis_size("wide")
    norb, depth, naux = gamma.shape
    width = naux // HALVES
    swap = [(d, d ^ 1) for d in range(count)]
    other = lax.ppermute(coefficients, "wide", swap)

    piece = []
    for j in range(HALVES):
        if j:
            gamma, place = lax.optimization_barrier((gamma, place))
        piece.append([gamma[i, :, j * width : (j + 1) * width] for i in range(norb)])
    shift = [
        [
            (2 * ring_chip(p) + k, 2 * ring_chip(p + way) + k)
            for p in range(GRID_CHIPS)
            for k in range(2)
        ]
        for way in WAYS
    ]
    arrived, sums, done = [], [], 0
    for t in range(GRID_CHIPS):
        arrived.append([list(part) for part in piece])
        if t + 1 == GRID_CHIPS:
            break
        for j in range(HALVES):
            while done < BEHIND[t][j]:
                sums = add_products(done, coefficients, other, arrived[done], sums)
                done += 1
            for i in range(norb):
                sent = piece[j][i]
                if t == 1 and i == j == 0:
                    sent, labels = lax.optimization_barrier((sent, labels))
                    ids = exchange(labels)
                if BEHIND[t][j]:
                    sent, sums = lax.optimization_barrier((sent, sums))
                piece[j][i] = lax.ppermute(sent, "wide", shift[i])
    while done < GRID_CHIPS - 1:
        sums = add_products(done, coefficients, other, arrived[done], sums)
        done += 1
    sums[:1], windows = add_products(
        done, coefficients, other, arrived[done][:1], sums[:1], keep=True
    )
    sums[1] = add_last_products(done, windows, arrived[done][1], sums[1])
    theirs = [lax.ppermute(sums[j][1], "wide", swap) for j in range(HALVES)]
    out = []
    for j in range(HALVES):
        out = [finish(j, place, sums[j][0], theirs[j], out, shape)]
    return store(ids), out[0]


def local(gamma, coefficients, owners):
    count = lax.axis_size("wide")
    blocks_here = owners.shape[0]
    slots = max(2, 2 * blocks_here // count)
    block_rows = coefficients.shape[0] // blocks_here
    norb, depth, naux = gamma.shape
    shape = (count, norb * block_rows, slots, naux)

    labels, place = routing(owners, count, slots, block_rows)
    if count == 2 * GRID_CHIPS and norb == len(WAYS):
        ids, out = ring_products(gamma, coefficients, labels, place, shape)
    else:
        gathered = lax.all_gather(gamma, "wide", axis=1, tiled=True)
        back = jnp.einsum(
            "ra,ian->irn", coefficients, gathered, preferred_element_type=jnp.float32
        ).astype(jnp.bfloat16)
        out = jnp.einsum("tr,irn->itn", place, back, preferred_element_type=jnp.float32)
        out = out.astype(jnp.bfloat16).reshape(norb, count, block_rows, slots, naux)
        out = out.transpose(1, 0, 2, 3, 4).reshape(shape)
        ids = exchange(labels)
    placed = exchange(out)
    return placed.transpose(0, 2, 1, 3)[None], ids[None]


def solution(mesh):
    placed = (P("groups", "wide", None), P("wide", None), P("wide", None))
    return jax.shard_map(
        local,
        mesh=mesh,
        in_specs=placed,
        out_specs=(P("wide", None, "groups", None, None), P("wide", "groups", None)),
        check_vma=False,
    )
```

```python
import functools
import math

import jax
import jax.numpy as jnp
from jax import lax
from jax.experimental import pallas as pl
from jax.experimental.pallas import tpu as pltpu
from jax.sharding import PartitionSpec as P

GRID_CHIPS = 8
HALVES = 2
BEHIND = ((0, 0), (0, 0), (0, 1), (1, 2), (2, 4), (4, 5), (5, 6))
WAYS = (1, -1)
LANES = 128
WINDOW = 896


def ring_chip(at):
    at = at % GRID_CHIPS
    back = 2 * ((GRID_CHIPS - at) % GRID_CHIPS)
    up = 2 * at - 1
    if isinstance(at, int):
        return up if 1 <= at <= GRID_CHIPS // 2 else back
    return jnp.where((at >= 1) & (at <= GRID_CHIPS // 2), up, back)


def ring_place(chip):
    z, y = chip // 2, chip % 2
    return jnp.where(y == 1, 1 + z, (GRID_CHIPS - z) % GRID_CHIPS)


def routing(owners, count, slots, block_rows):
    blocks_here = owners.shape[0]
    rows = blocks_here * block_rows
    owner_col = owners[:, 0]
    same = owner_col[:, None] == owner_col[None, :]
    lower = jnp.arange(blocks_here)[:, None] > jnp.arange(blocks_here)[None, :]
    rank = jnp.sum((same & lower).astype(jnp.int32), axis=1)
    target = owner_col * slots + rank
    select = jnp.arange(count * slots, dtype=jnp.int32)[:, None] == target[None, :]
    global_ids = lax.axis_index("wide") * blocks_here + jnp.arange(blocks_here, dtype=jnp.int32)
    labels = jnp.sum(jnp.where(select, global_ids[None, :] + 1, 0), axis=1) - 1
    row_at = jnp.arange(rows, dtype=jnp.int32)
    out_at = jnp.arange(count * block_rows * slots, dtype=jnp.int32)
    row_key = jnp.repeat(target, block_rows) * block_rows + row_at % block_rows
    out_key = (
        out_at // (block_rows * slots) * slots + out_at % slots
    ) * block_rows + out_at // slots % block_rows
    place = (out_key[:, None] == row_key[None, :]).astype(jnp.bfloat16)
    return labels.reshape(count, slots), place


def window_at(start, nvirt):
    return jnp.minimum(start // LANES * LANES, nvirt - WINDOW)


def step_kernel(t, parts, own_hbm, other_hbm, *refs):
    norb = len(WAYS)
    pieces = refs[: norb * parts]
    c_buf, g_buf, sems = refs[-3:]
    sums = refs[-3 - 2 * parts : -3]
    before = refs[norb * parts : -3 - 2 * parts]
    rows, nvirt = own_hbm.shape
    depth, width = pieces[0].shape
    me = lax.axis_index("wide")
    core = lax.rem(me, 2)
    here = ring_place(lax.div(me, 2))
    shifts, copies = [], []
    for i in range(norb):
        chip = ring_chip(here - t * WAYS[i] + GRID_CHIPS)
        start = (2 * chip + core) * depth
        at = pl.multiple_of(window_at(start, nvirt), LANES)
        shifts.append(pl.multiple_of(start - at, 16))
        columns = pl.ds(at, WINDOW)
        copies.append(
            [
                pltpu.make_async_copy(
                    source.at[:, columns], c_buf.at[i, pl.ds(k * rows, rows)], sems.at[i, k]
                )
                for k, source in enumerate((own_hbm, other_hbm))
            ]
        )
        for copy in copies[i]:
            copy.start()
    for i in range(norb):
        g_buf[i] = jnp.zeros_like(g_buf[i])
        for j in range(parts):
            g_buf[i, pl.ds(shifts[i], depth), pl.ds(j * width, width)] = pieces[
                j * norb + i
            ][...]
    for i in range(norb):
        for copy in copies[i]:
            copy.wait()
        for k in range(2):
            term = jnp.dot(
                c_buf[i, pl.ds(k * rows, rows)], g_buf[i], preferred_element_type=jnp.float32
            )
            for j in range(parts):
                part = term[:, j * width : (j + 1) * width]
                at = 2 * j + k
                sums[at][i] = before[at][i] + part if before else part


def last_kernel(t, c_ref, *refs):
    norb = len(WAYS)
    pieces, before, sums, g_buf = refs[:norb], refs[norb : norb + 2], refs[-3:-1], refs[-1]
    rows = before[0].shape[1]
    depth = pieces[0].shape[0]
    nvirt = depth * 2 * GRID_CHIPS
    me = lax.axis_index("wide")
    for i in range(norb):
        chip = ring_chip(ring_place(lax.div(me, 2)) - t * WAYS[i] + GRID_CHIPS)
        start = (2 * chip + lax.rem(me, 2)) * depth
        shift = pl.multiple_of(start - window_at(start, nvirt), 16)
        g_buf[i] = jnp.zeros_like(g_buf[i])
        g_buf[i, pl.ds(shift, depth), :] = pieces[i][...]
    for i in range(norb):
        for k in range(2):
            term = jnp.dot(
                c_ref[i, pl.ds(k * rows, rows)], g_buf[i], preferred_element_type=jnp.float32
            )
            sums[k][i] = before[k][i] + term


def add_last_products(t, windows, pieces, before):
    norb = len(WAYS)
    depth, width = pieces[0].shape
    vmem = pl.BlockSpec(memory_space=pltpu.VMEM)
    sums = jax.ShapeDtypeStruct(before[0].shape, jnp.float32)
    return pl.pallas_call(
        functools.partial(last_kernel, t),
        out_shape=[sums] * 2,
        in_specs=[vmem] * (1 + norb + 2),
        out_specs=[vmem] * 2,
        input_output_aliases={1 + norb + k: k for k in range(2)},
        scratch_shapes=[pltpu.VMEM((norb, WINDOW, width), jnp.bfloat16)],
        compiler_params=pltpu.CompilerParams(vmem_limit_bytes=20 << 20),
        cost_estimate=pl.CostEstimate(
            flops=2 * windows.size * width,
            bytes_accessed=2 * windows.size,
            transcendentals=0,
        ),
    )(windows, *pieces, *before)


def add_products(t, own, other, pieces, before, keep=False):
    rows, nvirt = own.shape
    parts, norb = len(pieces), len(WAYS)
    depth, width = pieces[0][0].shape
    sums = jax.ShapeDtypeStruct((norb, rows, width), jnp.float32)
    vmem = pl.BlockSpec(memory_space=pltpu.VMEM)
    hbm = pl.BlockSpec(memory_space=pltpu.HBM)
    flat = [piece for part in pieces for piece in part]
    old = [value for pair in before for value in pair]
    windows = (norb, 2 * rows, WINDOW)
    kept = [jax.ShapeDtypeStruct(windows, own.dtype)] * keep
    new = pl.pallas_call(
        functools.partial(step_kernel, t, parts),
        out_shape=[sums] * (2 * parts) + kept,
        in_specs=[hbm, hbm] + [vmem] * (len(flat) + len(old)),
        out_specs=[vmem] * (2 * parts + keep),
        input_output_aliases={2 + len(flat) + k: k for k in range(len(old))},
        scratch_shapes=[pltpu.VMEM(windows, own.dtype)] * (not keep)
        + [
            pltpu.VMEM((norb, WINDOW, parts * width), jnp.bfloat16),
            pltpu.SemaphoreType.DMA((norb, 2)),
        ],
        compiler_params=pltpu.CompilerParams(vmem_limit_bytes=20 << 20),
        cost_estimate=pl.CostEstimate(
            flops=4 * norb * rows * WINDOW * parts * width,
            bytes_accessed=4 * norb * rows * WINDOW,
            transcendentals=0,
        ),
    )(own, other, *flat, *old)
    pairs = [(new[2 * j], new[2 * j + 1]) for j in range(parts)]
    return (pairs, new[-1]) if keep else pairs


def finish_kernel(half, place_ref, mine_ref, theirs_ref, *refs):
    out_hbm, buf, sems = refs[-3:]
    norb, _, width = mine_ref.shape
    _, planes, slots, _ = out_hbm.shape
    columns = pl.ds(half * width, width)
    copies = []
    for i in range(norb):
        back = (mine_ref[i] + theirs_ref[i]).astype(jnp.bfloat16)
        out = jnp.dot(place_ref[...], back, preferred_element_type=jnp.float32)
        plane = pl.ds(i * (planes // norb), planes // norb)
        buf[:, plane] = out.astype(jnp.bfloat16).reshape(-1, planes // norb, slots, width)
        copies.append(
            pltpu.make_async_copy(
                buf.at[:, plane], out_hbm.at[:, plane, :, columns], sems.at[i]
            )
        )
        copies[i].start()
    for copy in copies:
        copy.wait()


def finish(half, place, mine, theirs, before, shape):
    vmem = pl.BlockSpec(memory_space=pltpu.VMEM)
    hbm = pl.BlockSpec(memory_space=pltpu.HBM)
    norb, _, width = mine.shape
    return pl.pallas_call(
        functools.partial(finish_kernel, half),
        out_shape=jax.ShapeDtypeStruct(shape, jnp.bfloat16),
        in_specs=[vmem] * 3 + [hbm] * len(before),
        out_specs=hbm,
        input_output_aliases={3: 0} if before else {},
        scratch_shapes=[
            pltpu.VMEM(shape[:3] + (width,), jnp.bfloat16),
            pltpu.SemaphoreType.DMA((norb,)),
        ],
        compiler_params=pltpu.CompilerParams(vmem_limit_bytes=20 << 20),
        cost_estimate=pl.CostEstimate(
            flops=math.prod(shape) * place.shape[1],
            bytes_accessed=2 * math.prod(shape),
            transcendentals=0,
        ),
    )(place, mine, theirs, *before)


def store_kernel(value_ref, out_hbm, sem):
    copy = pltpu.make_async_copy(value_ref, out_hbm, sem)
    copy.start()
    copy.wait()


def store(value):
    return pl.pallas_call(
        store_kernel,
        out_shape=jax.ShapeDtypeStruct(value.shape, value.dtype),
        in_specs=[pl.BlockSpec(memory_space=pltpu.VMEM)],
        out_specs=pl.BlockSpec(memory_space=pltpu.HBM),
        scratch_shapes=[pltpu.SemaphoreType.DMA],
    )(value)


def exchange(value):
    return lax.all_to_all(value, "wide", split_axis=0, concat_axis=0, tiled=True)


def ring_products(gamma, coefficients, labels, place, shape):
    count = lax.axis_size("wide")
    norb, depth, naux = gamma.shape
    width = naux // HALVES
    swap = [(d, d ^ 1) for d in range(count)]
    other = lax.ppermute(coefficients, "wide", swap)

    piece = []
    for j in range(HALVES):
        if j:
            gamma, labels, place = lax.optimization_barrier((gamma, labels, place))
            ids = exchange(labels)
        piece.append([gamma[i, :, j * width : (j + 1) * width] for i in range(norb)])
    shift = [
        [
            (2 * ring_chip(p) + k, 2 * ring_chip(p + way) + k)
            for p in range(GRID_CHIPS)
            for k in range(2)
        ]
        for way in WAYS
    ]
    arrived, sums, done = [], [], 0
    for t in range(GRID_CHIPS):
        arrived.append([list(part) for part in piece])
        if t + 1 == GRID_CHIPS:
            break
        for j in range(HALVES):
            while done < BEHIND[t][j]:
                sums = add_products(done, coefficients, other, arrived[done], sums)
                done += 1
            for i in range(norb):
                sent = piece[j][i]
                if t == 2 and i == j == 0:
                    sent, ids = lax.optimization_barrier((sent, ids))
                if BEHIND[t][j]:
                    sent, sums = lax.optimization_barrier((sent, sums))
                piece[j][i] = lax.ppermute(sent, "wide", shift[i])
    while done < GRID_CHIPS - 1:
        sums = add_products(done, coefficients, other, arrived[done], sums)
        done += 1
    sums[:1], windows = add_products(
        done, coefficients, other, arrived[done][:1], sums[:1], keep=True
    )
    sums[1] = add_last_products(done, windows, arrived[done][1], sums[1])
    theirs = [lax.ppermute(sums[j][1], "wide", swap) for j in range(HALVES)]
    out = []
    for j in range(HALVES):
        out = [finish(j, place, sums[j][0], theirs[j], out, shape)]
    return store(ids), out[0]


def local(gamma, coefficients, owners):
    count = lax.axis_size("wide")
    blocks_here = owners.shape[0]
    slots = max(2, 2 * blocks_here // count)
    block_rows = coefficients.shape[0] // blocks_here
    norb, depth, naux = gamma.shape
    shape = (count, norb * block_rows, slots, naux)

    labels, place = routing(owners, count, slots, block_rows)
    if count == 2 * GRID_CHIPS and norb == len(WAYS):
        ids, out = ring_products(gamma, coefficients, labels, place, shape)
    else:
        gathered = lax.all_gather(gamma, "wide", axis=1, tiled=True)
        back = jnp.einsum(
            "ra,ian->irn", coefficients, gathered, preferred_element_type=jnp.float32
        ).astype(jnp.bfloat16)
        out = jnp.einsum("tr,irn->itn", place, back, preferred_element_type=jnp.float32)
        out = out.astype(jnp.bfloat16).reshape(norb, count, block_rows, slots, naux)
        out = out.transpose(1, 0, 2, 3, 4).reshape(shape)
        ids = exchange(labels)
    placed = exchange(out)
    return placed.transpose(0, 2, 1, 3)[None], ids[None]


def solution(mesh):
    placed = (P("groups", "wide", None), P("wide", None), P("wide", None))
    return jax.shard_map(
        local,
        mesh=mesh,
        in_specs=placed,
        out_specs=(P("wide", None, "groups", None, None), P("wide", "groups", None)),
        check_vma=False,
    )
```

```python
import functools
import math

import jax
import jax.numpy as jnp
from jax import lax
from jax.experimental import pallas as pl
from jax.experimental.pallas import tpu as pltpu
from jax.sharding import PartitionSpec as P

GRID_CHIPS = 8
HALVES = 2
BEHIND = ((0, 0), (0, 0), (0, 1), (1, 2), (2, 4), (4, 5), (5, 6))
WAYS = (1, -1)
LANES = 128
WINDOW = 896


def ring_chip(at):
    at = at % GRID_CHIPS
    back = 2 * ((GRID_CHIPS - at) % GRID_CHIPS)
    up = 2 * at - 1
    if isinstance(at, int):
        return up if 1 <= at <= GRID_CHIPS // 2 else back
    return jnp.where((at >= 1) & (at <= GRID_CHIPS // 2), up, back)


def ring_place(chip):
    z, y = chip // 2, chip % 2
    return jnp.where(y == 1, 1 + z, (GRID_CHIPS - z) % GRID_CHIPS)


def routing(owners, count, slots, block_rows):
    blocks_here = owners.shape[0]
    rows = blocks_here * block_rows
    owner_col = owners[:, 0]
    same = owner_col[:, None] == owner_col[None, :]
    lower = jnp.arange(blocks_here)[:, None] > jnp.arange(blocks_here)[None, :]
    rank = jnp.sum((same & lower).astype(jnp.int32), axis=1)
    target = owner_col * slots + rank
    select = jnp.arange(count * slots, dtype=jnp.int32)[:, None] == target[None, :]
    global_ids = lax.axis_index("wide") * blocks_here + jnp.arange(blocks_here, dtype=jnp.int32)
    labels = jnp.sum(jnp.where(select, global_ids[None, :] + 1, 0), axis=1) - 1
    row_at = jnp.arange(rows, dtype=jnp.int32)
    out_at = jnp.arange(count * block_rows * slots, dtype=jnp.int32)
    row_key = jnp.repeat(target, block_rows) * block_rows + row_at % block_rows
    out_key = (
        out_at // (block_rows * slots) * slots + out_at % slots
    ) * block_rows + out_at // slots % block_rows
    place = (out_key[:, None] == row_key[None, :]).astype(jnp.bfloat16)
    return labels.reshape(count, slots), place


def window_at(start, nvirt):
    return jnp.minimum(start // LANES * LANES, nvirt - WINDOW)


def step_kernel(t, parts, own_hbm, other_hbm, *refs):
    norb = len(WAYS)
    pieces = refs[: norb * parts]
    c_buf, g_buf, sems = refs[-3:]
    sums = refs[-3 - 2 * parts : -3]
    before = refs[norb * parts : -3 - 2 * parts]
    rows, nvirt = own_hbm.shape
    depth, width = pieces[0].shape
    me = lax.axis_index("wide")
    core = lax.rem(me, 2)
    here = ring_place(lax.div(me, 2))
    shifts, copies = [], []
    for i in range(norb):
        chip = ring_chip(here - t * WAYS[i] + GRID_CHIPS)
        start = (2 * chip + core) * depth
        at = pl.multiple_of(window_at(start, nvirt), LANES)
        shifts.append(pl.multiple_of(start - at, 16))
        columns = pl.ds(at, WINDOW)
        copies.append(
            [
                pltpu.make_async_copy(
                    source.at[:, columns], c_buf.at[i, pl.ds(k * rows, rows)], sems.at[i, k]
                )
                for k, source in enumerate((own_hbm, other_hbm))
            ]
        )
        for copy in copies[i]:
            copy.start()
    for i in range(norb):
        g_buf[i] = jnp.zeros_like(g_buf[i])
        for j in range(parts):
            g_buf[i, pl.ds(shifts[i], depth), pl.ds(j * width, width)] = pieces[
                j * norb + i
            ][...]
    for i in range(norb):
        for copy in copies[i]:
            copy.wait()
        for k in range(2):
            term = jnp.dot(
                c_buf[i, pl.ds(k * rows, rows)], g_buf[i], preferred_element_type=jnp.float32
            )
            for j in range(parts):
                part = term[:, j * width : (j + 1) * width]
                at = 2 * j + k
                sums[at][i] = before[at][i] + part if before else part


def last_kernel(t, c_ref, *refs):
    norb = len(WAYS)
    pieces, before, sums, g_buf = refs[:norb], refs[norb : norb + 2], refs[-3:-1], refs[-1]
    rows = before[0].shape[1]
    depth = pieces[0].shape[0]
    nvirt = depth * 2 * GRID_CHIPS
    me = lax.axis_index("wide")
    for i in range(norb):
        chip = ring_chip(ring_place(lax.div(me, 2)) - t * WAYS[i] + GRID_CHIPS)
        start = (2 * chip + lax.rem(me, 2)) * depth
        shift = pl.multiple_of(start - window_at(start, nvirt), 16)
        g_buf[i] = jnp.zeros_like(g_buf[i])
        g_buf[i, pl.ds(shift, depth), :] = pieces[i][...]
    for i in range(norb):
        for k in range(2):
            term = jnp.dot(
                c_ref[i, pl.ds(k * rows, rows)], g_buf[i], preferred_element_type=jnp.float32
            )
            sums[k][i] = before[k][i] + term


def add_last_products(t, windows, pieces, before):
    norb = len(WAYS)
    depth, width = pieces[0].shape
    vmem = pl.BlockSpec(memory_space=pltpu.VMEM)
    sums = jax.ShapeDtypeStruct(before[0].shape, jnp.float32)
    return pl.pallas_call(
        functools.partial(last_kernel, t),
        out_shape=[sums] * 2,
        in_specs=[vmem] * (1 + norb + 2),
        out_specs=[vmem] * 2,
        input_output_aliases={1 + norb + k: k for k in range(2)},
        scratch_shapes=[pltpu.VMEM((norb, WINDOW, width), jnp.bfloat16)],
        compiler_params=pltpu.CompilerParams(vmem_limit_bytes=20 << 20),
        cost_estimate=pl.CostEstimate(
            flops=2 * windows.size * width,
            bytes_accessed=2 * windows.size,
            transcendentals=0,
        ),
    )(windows, *pieces, *before)


def add_products(t, own, other, pieces, before, keep=False):
    rows, nvirt = own.shape
    parts, norb = len(pieces), len(WAYS)
    depth, width = pieces[0][0].shape
    sums = jax.ShapeDtypeStruct((norb, rows, width), jnp.float32)
    vmem = pl.BlockSpec(memory_space=pltpu.VMEM)
    hbm = pl.BlockSpec(memory_space=pltpu.HBM)
    flat = [piece for part in pieces for piece in part]
    old = [value for pair in before for value in pair]
    windows = (norb, 2 * rows, WINDOW)
    kept = [jax.ShapeDtypeStruct(windows, own.dtype)] * keep
    new = pl.pallas_call(
        functools.partial(step_kernel, t, parts),
        out_shape=[sums] * (2 * parts) + kept,
        in_specs=[hbm, hbm] + [vmem] * (len(flat) + len(old)),
        out_specs=[vmem] * (2 * parts + keep),
        input_output_aliases={2 + len(flat) + k: k for k in range(len(old))},
        scratch_shapes=[pltpu.VMEM(windows, own.dtype)] * (not keep)
        + [
            pltpu.VMEM((norb, WINDOW, parts * width), jnp.bfloat16),
            pltpu.SemaphoreType.DMA((norb, 2)),
        ],
        compiler_params=pltpu.CompilerParams(vmem_limit_bytes=20 << 20),
        cost_estimate=pl.CostEstimate(
            flops=4 * norb * rows * WINDOW * parts * width,
            bytes_accessed=4 * norb * rows * WINDOW,
            transcendentals=0,
        ),
    )(own, other, *flat, *old)
    pairs = [(new[2 * j], new[2 * j + 1]) for j in range(parts)]
    return (pairs, new[-1]) if keep else pairs


def finish_kernel(half, place_ref, mine_ref, theirs_ref, *refs):
    out_hbm, buf, sems = refs[-3:]
    norb, _, width = mine_ref.shape
    _, _, planes, slots, _ = out_hbm.shape
    copies = []
    for i in range(norb):
        back = (mine_ref[i] + theirs_ref[i]).astype(jnp.bfloat16)
        out = jnp.dot(place_ref[...], back, preferred_element_type=jnp.float32)
        plane = pl.ds(i * (planes // norb), planes // norb)
        buf[:, plane] = out.astype(jnp.bfloat16).reshape(-1, planes // norb, slots, width)
        copies.append(
            pltpu.make_async_copy(buf.at[:, plane], out_hbm.at[:, half, plane], sems.at[i])
        )
        copies[i].start()
    for copy in copies:
        copy.wait()


def finish(half, place, mine, theirs, before, shape):
    vmem = pl.BlockSpec(memory_space=pltpu.VMEM)
    hbm = pl.BlockSpec(memory_space=pltpu.HBM)
    norb, _, width = mine.shape
    return pl.pallas_call(
        functools.partial(finish_kernel, half),
        out_shape=jax.ShapeDtypeStruct((shape[0], HALVES) + shape[1:3] + (width,), jnp.bfloat16),
        in_specs=[vmem] * 3 + [hbm] * len(before),
        out_specs=hbm,
        input_output_aliases={3: 0} if before else {},
        scratch_shapes=[
            pltpu.VMEM(shape[:3] + (width,), jnp.bfloat16),
            pltpu.SemaphoreType.DMA((norb,)),
        ],
        compiler_params=pltpu.CompilerParams(vmem_limit_bytes=20 << 20),
        cost_estimate=pl.CostEstimate(
            flops=math.prod(shape) * place.shape[1],
            bytes_accessed=2 * math.prod(shape),
            transcendentals=0,
        ),
    )(place, mine, theirs, *before)


def store_kernel(value_ref, out_hbm, sem):
    copy = pltpu.make_async_copy(value_ref, out_hbm, sem)
    copy.start()
    copy.wait()


def store(value):
    return pl.pallas_call(
        store_kernel,
        out_shape=jax.ShapeDtypeStruct(value.shape, value.dtype),
        in_specs=[pl.BlockSpec(memory_space=pltpu.VMEM)],
        out_specs=pl.BlockSpec(memory_space=pltpu.HBM),
        scratch_shapes=[pltpu.SemaphoreType.DMA],
    )(value)


def ring_products(gamma, coefficients, ids, place, shape):
    count = lax.axis_size("wide")
    norb, depth, naux = gamma.shape
    width = naux // HALVES
    swap = [(d, d ^ 1) for d in range(count)]
    other = lax.ppermute(coefficients, "wide", swap)

    piece = [
        [gamma[i, :, j * width : (j + 1) * width] for i in range(norb)] for j in range(HALVES)
    ]
    shift = [
        [
            (2 * ring_chip(p) + k, 2 * ring_chip(p + way) + k)
            for p in range(GRID_CHIPS)
            for k in range(2)
        ]
        for way in WAYS
    ]
    arrived, sums, done = [], [], 0
    for t in range(GRID_CHIPS):
        arrived.append([list(part) for part in piece])
        if t + 1 == GRID_CHIPS:
            break
        for j in range(HALVES):
            while done < BEHIND[t][j]:
                sums = add_products(done, coefficients, other, arrived[done], sums)
                done += 1
            for i in range(norb):
                sent = piece[j][i]
                if t == 2 and i == j == 0:
                    sent, ids, place = lax.optimization_barrier((sent, ids, place))
                if BEHIND[t][j]:
                    sent, sums = lax.optimization_barrier((sent, sums))
                piece[j][i] = lax.ppermute(sent, "wide", shift[i])
    while done < GRID_CHIPS - 1:
        sums = add_products(done, coefficients, other, arrived[done], sums)
        done += 1
    sums[:1], windows = add_products(
        done, coefficients, other, arrived[done][:1], sums[:1], keep=True
    )
    sums[1] = add_last_products(done, windows, arrived[done][1], sums[1])
    theirs = [lax.ppermute(sums[j][1], "wide", swap) for j in range(HALVES)]
    out = []
    for j in range(HALVES):
        out = [finish(j, place, sums[j][0], theirs[j], out, shape)]
    return store(ids), out[0]


def local(gamma, coefficients, owners):
    count = lax.axis_size("wide")
    blocks_here = owners.shape[0]
    slots = max(2, 2 * blocks_here // count)
    block_rows = coefficients.shape[0] // blocks_here
    norb, depth, naux = gamma.shape
    shape = (count, norb * block_rows, slots, naux)

    labels, place = routing(owners, count, slots, block_rows)
    ids = lax.all_to_all(labels, "wide", split_axis=0, concat_axis=0, tiled=True)
    if count == 2 * GRID_CHIPS and norb == len(WAYS):
        ids, out = ring_products(gamma, coefficients, ids, place, shape)
    else:
        gathered = lax.all_gather(gamma, "wide", axis=1, tiled=True)
        back = jnp.einsum(
            "ra,ian->irn", coefficients, gathered, preferred_element_type=jnp.float32
        ).astype(jnp.bfloat16)
        out = jnp.einsum("tr,irn->itn", place, back, preferred_element_type=jnp.float32)
        out = out.astype(jnp.bfloat16).reshape(norb, count, block_rows, slots, naux)
        out = out.transpose(1, 0, 2, 3, 4).reshape(shape)
    placed = lax.all_to_all(out, "wide", split_axis=0, concat_axis=0, tiled=True)
    if placed.ndim > len(shape):
        placed = placed.transpose(0, 2, 3, 1, 4).reshape(shape)
    return placed.transpose(0, 2, 1, 3)[None], ids[None]


def solution(mesh):
    placed = (P("groups", "wide", None), P("wide", None), P("wide", None))
    return jax.shard_map(
        local,
        mesh=mesh,
        in_specs=placed,
        out_specs=(P("wide", None, "groups", None, None), P("wide", "groups", None)),
        check_vma=False,
    )
```

```python
import functools
import math

import jax
import jax.numpy as jnp
from jax import lax
from jax.experimental import pallas as pl
from jax.experimental.pallas import tpu as pltpu
from jax.sharding import PartitionSpec as P

GRID_CHIPS = 8
HALVES = 2
BEHIND = ((0, 0), (0, 0), (0, 1), (1, 2), (2, 4), (4, 5), (5, 6))
WAYS = (-1, 1)
LANES = 128
WINDOW = 896


def ring_chip(at):
    at = at % GRID_CHIPS
    back = 2 * ((GRID_CHIPS - at) % GRID_CHIPS)
    up = 2 * at - 1
    if isinstance(at, int):
        return up if 1 <= at <= GRID_CHIPS // 2 else back
    return jnp.where((at >= 1) & (at <= GRID_CHIPS // 2), up, back)


def ring_place(chip):
    z, y = chip // 2, chip % 2
    return jnp.where(y == 1, 1 + z, (GRID_CHIPS - z) % GRID_CHIPS)


def routing(owners, count, slots, block_rows):
    blocks_here = owners.shape[0]
    rows = blocks_here * block_rows
    owner_col = owners[:, 0]
    same = owner_col[:, None] == owner_col[None, :]
    lower = jnp.arange(blocks_here)[:, None] > jnp.arange(blocks_here)[None, :]
    rank = jnp.sum((same & lower).astype(jnp.int32), axis=1)
    target = owner_col * slots + rank
    select = jnp.arange(count * slots, dtype=jnp.int32)[:, None] == target[None, :]
    global_ids = lax.axis_index("wide") * blocks_here + jnp.arange(blocks_here, dtype=jnp.int32)
    labels = jnp.sum(jnp.where(select, global_ids[None, :] + 1, 0), axis=1) - 1
    row_at = jnp.arange(rows, dtype=jnp.int32)
    out_at = jnp.arange(count * block_rows * slots, dtype=jnp.int32)
    row_key = jnp.repeat(target, block_rows) * block_rows + row_at % block_rows
    out_key = (
        out_at // (block_rows * slots) * slots + out_at % slots
    ) * block_rows + out_at // slots % block_rows
    place = (out_key[:, None] == row_key[None, :]).astype(jnp.bfloat16)
    return labels.reshape(count, slots), place


def window_at(start, nvirt):
    return jnp.minimum(start // LANES * LANES, nvirt - WINDOW)


def step_kernel(t, parts, own_hbm, other_hbm, *refs):
    norb = len(WAYS)
    pieces = refs[: norb * parts]
    c_buf, g_buf, sems = refs[-3:]
    sums = refs[-3 - 2 * parts : -3]
    before = refs[norb * parts : -3 - 2 * parts]
    rows, nvirt = own_hbm.shape
    depth, width = pieces[0].shape
    me = lax.axis_index("wide")
    core = lax.rem(me, 2)
    here = ring_place(lax.div(me, 2))
    shifts, copies = [], []
    for i in range(norb):
        chip = ring_chip(here - t * WAYS[i] + GRID_CHIPS)
        start = (2 * chip + core) * depth
        at = pl.multiple_of(window_at(start, nvirt), LANES)
        shifts.append(pl.multiple_of(start - at, 16))
        columns = pl.ds(at, WINDOW)
        copies.append(
            [
                pltpu.make_async_copy(
                    source.at[:, columns], c_buf.at[i, pl.ds(k * rows, rows)], sems.at[i, k]
                )
                for k, source in enumerate((own_hbm, other_hbm))
            ]
        )
        for copy in copies[i]:
            copy.start()
    for i in range(norb):
        g_buf[i] = jnp.zeros_like(g_buf[i])
        for j in range(parts):
            g_buf[i, pl.ds(shifts[i], depth), pl.ds(j * width, width)] = pieces[
                j * norb + i
            ][...]
    for i in range(norb):
        for copy in copies[i]:
            copy.wait()
        for k in range(2):
            term = jnp.dot(
                c_buf[i, pl.ds(k * rows, rows)], g_buf[i], preferred_element_type=jnp.float32
            )
            for j in range(parts):
                part = term[:, j * width : (j + 1) * width]
                at = 2 * j + k
                sums[at][i] = before[at][i] + part if before else part


def last_kernel(t, c_ref, *refs):
    norb = len(WAYS)
    pieces, before, sums, g_buf = refs[:norb], refs[norb : norb + 2], refs[-3:-1], refs[-1]
    rows = before[0].shape[1]
    depth = pieces[0].shape[0]
    nvirt = depth * 2 * GRID_CHIPS
    me = lax.axis_index("wide")
    for i in range(norb):
        chip = ring_chip(ring_place(lax.div(me, 2)) - t * WAYS[i] + GRID_CHIPS)
        start = (2 * chip + lax.rem(me, 2)) * depth
        shift = pl.multiple_of(start - window_at(start, nvirt), 16)
        g_buf[i] = jnp.zeros_like(g_buf[i])
        g_buf[i, pl.ds(shift, depth), :] = pieces[i][...]
    for i in range(norb):
        for k in range(2):
            term = jnp.dot(
                c_ref[i, pl.ds(k * rows, rows)], g_buf[i], preferred_element_type=jnp.float32
            )
            sums[k][i] = before[k][i] + term


def add_last_products(t, windows, pieces, before):
    norb = len(WAYS)
    depth, width = pieces[0].shape
    vmem = pl.BlockSpec(memory_space=pltpu.VMEM)
    sums = jax.ShapeDtypeStruct(before[0].shape, jnp.float32)
    return pl.pallas_call(
        functools.partial(last_kernel, t),
        out_shape=[sums] * 2,
        in_specs=[vmem] * (1 + norb + 2),
        out_specs=[vmem] * 2,
        input_output_aliases={1 + norb + k: k for k in range(2)},
        scratch_shapes=[pltpu.VMEM((norb, WINDOW, width), jnp.bfloat16)],
        compiler_params=pltpu.CompilerParams(vmem_limit_bytes=20 << 20),
        cost_estimate=pl.CostEstimate(
            flops=2 * windows.size * width,
            bytes_accessed=2 * windows.size,
            transcendentals=0,
        ),
    )(windows, *pieces, *before)


def add_products(t, own, other, pieces, before, keep=False):
    rows, nvirt = own.shape
    parts, norb = len(pieces), len(WAYS)
    depth, width = pieces[0][0].shape
    sums = jax.ShapeDtypeStruct((norb, rows, width), jnp.float32)
    vmem = pl.BlockSpec(memory_space=pltpu.VMEM)
    hbm = pl.BlockSpec(memory_space=pltpu.HBM)
    flat = [piece for part in pieces for piece in part]
    old = [value for pair in before for value in pair]
    windows = (norb, 2 * rows, WINDOW)
    kept = [jax.ShapeDtypeStruct(windows, own.dtype)] * keep
    new = pl.pallas_call(
        functools.partial(step_kernel, t, parts),
        out_shape=[sums] * (2 * parts) + kept,
        in_specs=[hbm, hbm] + [vmem] * (len(flat) + len(old)),
        out_specs=[vmem] * (2 * parts + keep),
        input_output_aliases={2 + len(flat) + k: k for k in range(len(old))},
        scratch_shapes=[pltpu.VMEM(windows, own.dtype)] * (not keep)
        + [
            pltpu.VMEM((norb, WINDOW, parts * width), jnp.bfloat16),
            pltpu.SemaphoreType.DMA((norb, 2)),
        ],
        compiler_params=pltpu.CompilerParams(vmem_limit_bytes=20 << 20),
        cost_estimate=pl.CostEstimate(
            flops=4 * norb * rows * WINDOW * parts * width,
            bytes_accessed=4 * norb * rows * WINDOW,
            transcendentals=0,
        ),
    )(own, other, *flat, *old)
    pairs = [(new[2 * j], new[2 * j + 1]) for j in range(parts)]
    return (pairs, new[-1]) if keep else pairs


def finish_kernel(half, place_ref, mine_ref, theirs_ref, *refs):
    out_hbm, buf, sems = refs[-3:]
    norb, _, width = mine_ref.shape
    _, _, planes, slots, _ = out_hbm.shape
    copies = []
    for i in range(norb):
        back = (mine_ref[i] + theirs_ref[i]).astype(jnp.bfloat16)
        out = jnp.dot(place_ref[...], back, preferred_element_type=jnp.float32)
        plane = pl.ds(i * (planes // norb), planes // norb)
        buf[:, plane] = out.astype(jnp.bfloat16).reshape(-1, planes // norb, slots, width)
        copies.append(
            pltpu.make_async_copy(buf.at[:, plane], out_hbm.at[:, half, plane], sems.at[i])
        )
        copies[i].start()
    for copy in copies:
        copy.wait()


def finish(half, place, mine, theirs, before, shape):
    vmem = pl.BlockSpec(memory_space=pltpu.VMEM)
    hbm = pl.BlockSpec(memory_space=pltpu.HBM)
    norb, _, width = mine.shape
    return pl.pallas_call(
        functools.partial(finish_kernel, half),
        out_shape=jax.ShapeDtypeStruct((shape[0], HALVES) + shape[1:3] + (width,), jnp.bfloat16),
        in_specs=[vmem] * 3 + [hbm] * len(before),
        out_specs=hbm,
        input_output_aliases={3: 0} if before else {},
        scratch_shapes=[
            pltpu.VMEM(shape[:3] + (width,), jnp.bfloat16),
            pltpu.SemaphoreType.DMA((norb,)),
        ],
        compiler_params=pltpu.CompilerParams(vmem_limit_bytes=20 << 20),
        cost_estimate=pl.CostEstimate(
            flops=math.prod(shape) * place.shape[1],
            bytes_accessed=2 * math.prod(shape),
            transcendentals=0,
        ),
    )(place, mine, theirs, *before)


def store_kernel(value_ref, out_hbm, sem):
    copy = pltpu.make_async_copy(value_ref, out_hbm, sem)
    copy.start()
    copy.wait()


def store(value):
    return pl.pallas_call(
        store_kernel,
        out_shape=jax.ShapeDtypeStruct(value.shape, value.dtype),
        in_specs=[pl.BlockSpec(memory_space=pltpu.VMEM)],
        out_specs=pl.BlockSpec(memory_space=pltpu.HBM),
        scratch_shapes=[pltpu.SemaphoreType.DMA],
    )(value)


def ring_products(gamma, coefficients, ids, place, shape):
    count = lax.axis_size("wide")
    norb, depth, naux = gamma.shape
    width = naux // HALVES
    swap = [(d, d ^ 1) for d in range(count)]
    other = lax.ppermute(coefficients, "wide", swap)

    piece = [
        [gamma[i, :, j * width : (j + 1) * width] for i in range(norb)] for j in range(HALVES)
    ]
    shift = [
        [
            (2 * ring_chip(p) + k, 2 * ring_chip(p + way) + k)
            for p in range(GRID_CHIPS)
            for k in range(2)
        ]
        for way in WAYS
    ]
    arrived, sums, done = [], [], 0
    for t in range(GRID_CHIPS):
        arrived.append([list(part) for part in piece])
        if t + 1 == GRID_CHIPS:
            break
        for j in range(HALVES):
            while done < BEHIND[t][j]:
                sums = add_products(done, coefficients, other, arrived[done], sums)
                done += 1
            for i in range(norb):
                sent = piece[j][i]
                if t == 2 and i == j == 0:
                    sent, ids, place = lax.optimization_barrier((sent, ids, place))
                if BEHIND[t][j]:
                    sent, sums = lax.optimization_barrier((sent, sums))
                piece[j][i] = lax.ppermute(sent, "wide", shift[i])
    while done < GRID_CHIPS - 1:
        sums = add_products(done, coefficients, other, arrived[done], sums)
        done += 1
    sums[:1], windows = add_products(
        done, coefficients, other, arrived[done][:1], sums[:1], keep=True
    )
    sums[1] = add_last_products(done, windows, arrived[done][1], sums[1])
    theirs = [lax.ppermute(sums[j][1], "wide", swap) for j in range(HALVES)]
    out = []
    for j in range(HALVES):
        out = [finish(j, place, sums[j][0], theirs[j], out, shape)]
    return store(ids), out[0]


def local(gamma, coefficients, owners):
    count = lax.axis_size("wide")
    blocks_here = owners.shape[0]
    slots = max(2, 2 * blocks_here // count)
    block_rows = coefficients.shape[0] // blocks_here
    norb, depth, naux = gamma.shape
    shape = (count, norb * block_rows, slots, naux)

    labels, place = routing(owners, count, slots, block_rows)
    ids = lax.all_to_all(labels, "wide", split_axis=0, concat_axis=0, tiled=True)
    if count == 2 * GRID_CHIPS and norb == len(WAYS):
        ids, out = ring_products(gamma, coefficients, ids, place, shape)
    else:
        gathered = lax.all_gather(gamma, "wide", axis=1, tiled=True)
        back = jnp.einsum(
            "ra,ian->irn", coefficients, gathered, preferred_element_type=jnp.float32
        ).astype(jnp.bfloat16)
        out = jnp.einsum("tr,irn->itn", place, back, preferred_element_type=jnp.float32)
        out = out.astype(jnp.bfloat16).reshape(norb, count, block_rows, slots, naux)
        out = out.transpose(1, 0, 2, 3, 4).reshape(shape)
    placed = lax.all_to_all(out, "wide", split_axis=0, concat_axis=0, tiled=True)
    if placed.ndim > len(shape):
        placed = placed.transpose(0, 2, 3, 1, 4).reshape(shape)
    return placed.transpose(0, 2, 1, 3)[None], ids[None]


def solution(mesh):
    placed = (P("groups", "wide", None), P("wide", None), P("wide", None))
    return jax.shard_map(
        local,
        mesh=mesh,
        in_specs=placed,
        out_specs=(P("wide", None, "groups", None, None), P("wide", "groups", None)),
        check_vma=False,
    )
```
